32 devices in a mesh: dp: 4 (over z), ctx: 8 (over y, x, core).
Axes of the slice: x: 2, y: 2, z: 4, core: 2. Of those that a mesh axis runs over, the one named last changes fastest.
Arguments:
- queries: bfloat16 [4, 1024, 1024], P('dp', 'ctx'), may hold values from -6 to 6
- key_in: bfloat16 [4, 1024, 1024], P('dp', 'ctx'), may hold values from -6 to 6
- value_in: bfloat16 [4, 1024, 2048], P('dp', 'ctx'), may hold values from -6 to 6
- gate_in: bfloat16 [4, 1024, 2048], P('dp', 'ctx'), may hold values from -6 to 6
- residual_in: bfloat16 [4, 1024, 2048], P('dp', 'ctx'), may hold values from -6 to 6
- log_decay: float32 [4, 16, 1024], P('dp', None, 'ctx'), may hold values from -1 to 0
- beta_logit: float32 [4, 16, 1024], P('dp', None, 'ctx'), may hold values from -6 to 6
- lengths: int32 [4, 4], P('dp'), may hold values from 1 to 512, 1024 in all within a row
- head_gain: float32 [128], replicated, may hold values from 0.1 to 1.9
- out_proj: bfloat16 [2048, 2048], replicated, may hold values from -0.125 to 0.125
- post_gain: float32 [2048], replicated, may hold values from 0.1 to 1.9
- expert_in: bfloat16 [64, 2048, 1024], P(('dp', 'ctx')), may hold values from -0.125 to 0.125
- expert_out: bfloat16 [64, 512, 2048], P(('dp', 'ctx')), may hold values from -0.25 to 0.25
- routes: int32 [4, 1024, 10], P('dp', 'ctx'), may hold values from 0 to 63, all different within a row; in each aligned block of 128 rows (0 to 127, 128 to 255, ..., all dimensions but the last counted through in order) at most 24 rows name the same one
- route_gates: float32 [4, 1024, 10], P('dp', 'ctx'), may hold values from 0.05 to 0.25
Outputs:
- layer_out: bfloat16 [4, 1024, 2048], P('dp', 'ctx')
The draws below stay inside these ranges and needn't reach their ends.
Inputs may be any that keep to these rules, and one draw needn't show every extreme that they name: `routes`: each row names 10 different experts; among the rows of one device (aligned blocks of 128 positions) no expert is named more than 24 times, a bound that some block reaches. The lengths of a pack sum to 1024.
All inputs are finite; a program needn't handle non-finite values.
Results may differ from the reference program's by a relative error of at most 0.014.
Values may be sent and summed in bfloat16 or wider, within the bound.
A program may use at most 256 MiB of HBM per device.

```python
import math
import jax
import jax.numpy as jnp
import numpy as np
from jax import lax

D = 2048
DK = 128
DV = 128
FF = 512
TOPK = 10
HK = 8
HV = 16
BLOCK = 64
NDOC = 4
TOK_DEV = 128
PACK_POSITIONS = 1024
PACKS = 4
EXPERTS = 64
CAP = 24
N_DP = 4
N_CTX = 8


def draw_log_decay(key, part):
    key = jax.random.fold_in(key, 7)
    variety_option_key, rate_option_key, jitter_option_key, block_option_key, spike_option_key, depth_option_key = jax.random.split(key, 6)
    tensor_extent = (PACKS, HV, PACK_POSITIONS)
    fast_share = 0.5
    fast_head = jax.random.uniform(variety_option_key, (PACKS, HV, 1)) < fast_share
    spread = jnp.exp(jax.random.uniform(rate_option_key, (PACKS, HV, 1), minval=0.0, maxval=math.log(2.0)))
    baseline_rate = jnp.where(fast_head, 1.0 / 40.0, 0.5 * math.log(10.0) / PACK_POSITIONS) * spread
    block_count = PACK_POSITIONS // TOK_DEV
    block_multiplier = jnp.exp(jax.random.uniform(block_option_key, (PACKS, HV, block_count, 1), minval=0.0, maxval=math.log(2.0)))
    block_multiplier = jnp.broadcast_to(block_multiplier, (PACKS, HV, block_count, TOK_DEV)).reshape(tensor_extent)
    jitter_level = jnp.exp(jax.random.uniform(jitter_option_key, tensor_extent, minval=math.log(0.5), maxval=math.log(1.5)))
    spike_train = jax.random.uniform(spike_option_key, tensor_extent) < 3.0 / PACK_POSITIONS
    spike_depth = jax.random.uniform(depth_option_key, tensor_extent, minval=0.22, maxval=0.69)
    return -(baseline_rate * block_multiplier * jitter_level) - jnp.where(spike_train, spike_depth, 0.0)


def block_levels(rng, extent, pieces, smallest, high):
    factor_of = 1.0
    for axis_at, parts in pieces:
        draws = jax.random.uniform(jax.random.fold_in(jax.random.fold_in(rng, 6), axis_at), (parts,), jnp.float32, smallest / len(pieces), high / len(pieces))
        factor_of = factor_of * jnp.repeat(jnp.exp(draws), extent[axis_at] // parts).reshape((-1,) + (1,) * (len(extent) - 1 - axis_at))
    return factor_of


def split_up(number_of, total, limit, lean):
    weights = [(1 << 20) // math.isqrt(rank ** lean) + 1 for rank in range(2, number_of + 1)]
    rest, counts = total - limit - (number_of - 1), [1] * (number_of - 1)
    while rest > 0:
        free = [i for i in range(number_of - 1) if counts[i] < limit]
        mass, left = sum([weights[i] for i in free]), rest
        for i in free:
            more = min(limit - counts[i], max(1, left * weights[i] // mass), rest)
            counts[i] = counts[i] + more
            rest = rest - more
    return np.array([limit] + counts)


def uneven_parts(own_key, amount, total, reach, lean):
    if amount == 2:
        one = jax.random.randint(own_key, (), max(1, total - reach), min(reach, total - 1) + 1)
        return jnp.stack([one, total - one])
    tallies = jnp.asarray(split_up(amount, total, reach, lean), jnp.int32)
    pairs = (amount - 1) // 2
    giver, sink = tallies[1:1 + 2 * pairs:2], tallies[2:2 + 2 * pairs:2]
    slack = jnp.minimum(giver - 1, reach - sink)
    moved = jax.random.randint(jax.random.fold_in(own_key, 1), (pairs,), 0, 1 << 20) % (slack + 1)
    tallies = tallies.at[1:1 + 2 * pairs:2].set(giver - moved).at[2:2 + 2 * pairs:2].set(sink + moved)
    return tallies[jax.random.permutation(jax.random.fold_in(own_key, 2), amount)]


def routed_block(rng, own, number, rows, number_of, top, most, slope):
    order = jax.random.permutation(rng, number_of)
    heavy_load, ordinary = portions_of(number_of, rows * top, most, slope, True), portions_of(number_of, rows * top, most, slope, False)
    places = jnp.arange(number_of)

    def named(sizes, offset_by):
        used = int((sizes > 0).sum())
        fixed = max(1, used // 4)
        passed = fixed + (places - fixed + offset_by * (used - fixed)) % max(1, number_of - fixed)
        return jnp.zeros((number_of,), jnp.int32).at[order[jnp.where(places < fixed, places, passed)]].set(jnp.asarray(sizes, jnp.int32))

    sizes = jnp.where(number % 4 == 0, named(heavy_load, number // 4), named(ordinary, number - number // 4 - 1))
    mixed = jax.random.permutation(jax.random.fold_in(own, 3), number_of)
    source_of, taker = mixed[0:number_of // 2 * 2:2], mixed[1:number_of // 2 * 2:2]
    room = jnp.minimum(sizes[source_of] - 1, most - sizes[taker]) // 2
    room = jnp.where((source_of == order[0]) | (taker == order[0]) | (sizes[taker] == 0), 0, jnp.maximum(room, 0))
    passed = jax.random.randint(jax.random.fold_in(own, 4), (number_of // 2,), 0, 1 << 20) % (room + 1)
    sizes = sizes.at[source_of].add(-passed).at[taker].add(passed)
    members = jnp.searchsorted(jnp.cumsum(sizes), jnp.arange(rows * top), side="right").astype(jnp.int32)
    grid = members.reshape(top, rows).T
    grid = grid[jax.random.permutation(jax.random.fold_in(own, 1), rows)]
    offset_by = jax.random.randint(jax.random.fold_in(own, 2), (rows, 1), 0, top)
    return jnp.take_along_axis(grid, (jnp.arange(top)[None, :] + offset_by) % top, axis=1)


def portions_of(count, total, limit, lean, full):
    loads = [(1 << 20) // math.isqrt(standing ** lean) + 1 for standing in range(1, count + 1)]
    largest = limit if full else min(limit, max(-(-total // count), total * loads[0] // sum(loads)))
    least = 1 if total - largest >= count - 1 else 0
    given, spare = [largest] + [least] * (count - 1), total - largest - least * (count - 1)
    while spare > 0:
        free = [i for i in range(1, count) if given[i] < largest] or [i for i in range(1, count) if given[i] < limit]
        pool, left = sum([loads[i] for i in free]), spare
        for i in free:
            extra = min(limit - given[i], max(1, left * loads[i] // pool), spare)
            given[i] = given[i] + extra
            spare = spare - extra
    return np.array(given)


def normal_values(own_key, extent, width, most, cuts=(), kind=jnp.bfloat16):
    values = width * jax.random.normal(own_key, extent, jnp.float32)
    if cuts:
        values = values * block_levels(own_key, extent, cuts, -0.22, 0.18)
    return jnp.clip(values, -most, most).astype(kind)


def setup_inputs(seed: int = 0) -> dict:
    streams_of = jax.random.split(jax.random.key(seed), 16)
    queries = normal_values(streams_of[0], (PACKS, PACK_POSITIONS, HK * DK), 1.0, 6.0, ((0, 4), (1, 8)))
    key_in = normal_values(streams_of[1], (PACKS, PACK_POSITIONS, HK * DK), 1.0, 6.0, ((0, 4), (1, 8)))
    value_in = normal_values(streams_of[2], (PACKS, PACK_POSITIONS, HV * DV), 1.0, 6.0, ((0, 4), (1, 8)))
    gate_in = normal_values(streams_of[3], (PACKS, PACK_POSITIONS, HV * DV), 1.0, 6.0, ((0, 4), (1, 8)))
    residual_in = normal_values(streams_of[4], (PACKS, PACK_POSITIONS, D), 1.0, 6.0, ((0, 4), (1, 8)))
    log_decay = draw_log_decay(jax.random.fold_in(streams_of[15], 71), 0)
    beta_logit = normal_values(streams_of[6], (PACKS, HV, PACK_POSITIONS), 1.5, 6.0, ((0, 4), (2, 8)), jnp.float32)
    lengths = jax.vmap(lambda own: uneven_parts(own, NDOC, PACK_POSITIONS, PACK_POSITIONS // 2, 2))(jax.random.split(streams_of[7], PACKS)).reshape((PACKS, NDOC)).astype(jnp.int32)
    head_gain = jnp.clip(1.0 + 0.18 * jax.random.normal(streams_of[8], (DV,), jnp.float32), 0.1, 1.9)
    out_proj = normal_values(streams_of[9], (HV * DV, D), (HV * DV) ** -0.5, 0.125)
    post_gain = jnp.clip(1.0 + 0.18 * jax.random.normal(streams_of[10], (D,), jnp.float32), 0.1, 1.9)
    expert_in = normal_values(streams_of[11], (EXPERTS, D, 2 * FF), D ** -0.5, 0.125, ((0, 32),))
    expert_out = normal_values(streams_of[12], (EXPERTS, FF, D), FF ** -0.5, 0.25, ((0, 32),))
    routes_keys = jax.random.split(jax.random.fold_in(streams_of[13], 1), PACKS * PACK_POSITIONS // TOK_DEV)
    routes_turns = jax.random.permutation(jax.random.fold_in(streams_of[13], 3), PACKS * PACK_POSITIONS // TOK_DEV)
    routes = jax.vmap(lambda own, number: routed_block(jax.random.fold_in(streams_of[13], 2), own, number, TOK_DEV, EXPERTS, TOPK, CAP, 2))(routes_keys, routes_turns).reshape((PACKS, PACK_POSITIONS, TOPK))
    route_gates = jnp.clip(0.05 + 0.2 * jax.random.uniform(streams_of[14], (PACKS, PACK_POSITIONS, TOPK), jnp.float32) ** block_levels(streams_of[14], (PACKS, PACK_POSITIONS, TOPK), ((0, 4), (1, 8)), -0.2, 0.2), 0.05, 0.25)
    return dict(queries=queries, key_in=key_in, value_in=value_in, gate_in=gate_in, residual_in=residual_in, log_decay=log_decay, beta_logit=beta_logit, lengths=lengths, head_gain=head_gain, out_proj=out_proj, post_gain=post_gain, expert_in=expert_in, expert_out=expert_out, routes=routes, route_gates=route_gates)


EPSILON = 1e-06
HIGHEST = lax.Precision.HIGHEST
ROWWISE = lax.Precision.HIGH

def unit_heads(matrix, head_count, factor):
    shaped = matrix.astype(jnp.float32).reshape(matrix.shape[0], head_count, -1)
    return shaped * lax.rsqrt(lax.optimization_barrier(jnp.sum(shaped * shaped, -1, keepdims=True)) + EPSILON) * factor

def segment_of(lengths, positions):
    starts = jnp.cumsum(lengths) - lengths
    return lax.optimization_barrier(jnp.sum((starts[:, None] <= positions[None, :]).astype(jnp.int32), 0)) - 1

def block_terms(queries, key_rows, value_rows, beta_gate, decay_log, segment, seg_before):
    length = key_rows.shape[1]
    cumulative = jnp.cumsum(decay_log, axis=-1)
    rows_at = jnp.arange(length)[:, None]
    cols_at = jnp.arange(length)[None, :]
    same_doc = (segment[:, None] == segment[None, :]) & (rows_at >= cols_at)
    log_gap = jnp.minimum(cumulative[:, :, None] - cumulative[:, None, :], 0.0)
    decay_pair = jnp.where(same_doc[None], jnp.exp(log_gap), 0.0)
    from_start = jnp.where((segment == seg_before)[None, :], jnp.exp(cumulative), 0.0)
    to_end = decay_pair[:, -1, :]
    key_inner = jnp.einsum('hcd,hsd->hcs', key_rows, key_rows, precision=ROWWISE)
    lower_part = jnp.where((rows_at > cols_at)[None], beta_gate[:, :, None] * decay_pair * key_inner, 0.0)
    system = jnp.eye(length, dtype=jnp.float32)[None] + lower_part
    right_side = jnp.concatenate([beta_gate[:, :, None] * value_rows, (beta_gate * from_start)[:, :, None] * key_rows], axis=-1)
    solved = jax.scipy.linalg.solve_triangular(system, right_side, lower=True, unit_diagonal=True)
    value_width = value_rows.shape[-1]
    pseudo = solved[..., :value_width]
    weights = solved[..., value_width:]
    scores = jnp.einsum('hcd,hsd->hcs', queries, key_rows, precision=ROWWISE) * decay_pair
    weighted = key_rows * to_end[:, :, None]
    key_width = key_rows.shape[-1]
    transition = from_start[:, -1][:, None, None] * jnp.eye(key_width, dtype=jnp.float32)[None] - jnp.einsum('hcd,hce->hde', weighted, weights, precision=HIGHEST)
    offset = jnp.einsum('hcd,hce->hde', weighted, pseudo, precision=HIGHEST)
    return (pseudo, weights, scores, from_start, transition, offset)

def block_output(queries, pseudo, weights, scores, from_start, carried):
    errors = pseudo - jnp.einsum('hcd,hde->hce', weights, carried, precision=ROWWISE)
    return jnp.einsum('hcd,hde->hce', queries * from_start[:, :, None], carried, precision=ROWWISE) + jnp.einsum('hcs,hse->hce', scores, errors, precision=ROWWISE)

def apply_map(transition, carried):
    return jnp.einsum('hde,hef->hdf', transition, carried, precision=HIGHEST)

def head_blocks(matrix, block_len):
    length, head_count, inner_width = matrix.shape
    return matrix.reshape(length // block_len, block_len, head_count, inner_width).transpose(0, 2, 1, 3)

def prepare(queries, key_in, value_in, log_decay, beta_logit, segment, seg_before):
    length = queries.shape[0]
    group_size = HV // HK
    query_heads = jnp.repeat(unit_heads(queries, HK, DK ** (-0.5)), group_size, axis=1)
    key_heads = jnp.repeat(unit_heads(key_in, HK, 1.0), group_size, axis=1)
    value_heads = value_in.astype(jnp.float32).reshape(length, HV, DV)
    nblock = length // BLOCK
    beta_gate = jax.nn.sigmoid(beta_logit).reshape(HV, nblock, BLOCK).transpose(1, 0, 2)
    decay_log = log_decay.reshape(HV, nblock, BLOCK).transpose(1, 0, 2)
    seg_blocks = segment.reshape(nblock, BLOCK)
    seg_starts = jnp.concatenate([jnp.reshape(seg_before, (1,)).astype(jnp.int32), seg_blocks[:-1, -1]])
    query_blocks = head_blocks(query_heads, BLOCK)
    terms = jax.vmap(block_terms)(query_blocks, head_blocks(key_heads, BLOCK), head_blocks(value_heads, BLOCK), beta_gate, decay_log, seg_blocks, seg_starts)
    return (query_blocks, terms)

def finish(query_blocks, terms, start_state, gate_in, residual_in, head_gain, out_proj):
    pseudo, weights, scores, from_start, transition, offset = terms

    def advance(carried, member):
        return (apply_map(member[0], carried) + member[1], carried)
    final_state, block_starts = lax.scan(advance, start_state, (transition, offset))
    outputs = jax.vmap(block_output)(query_blocks, pseudo, weights, scores, from_start, block_starts)
    length = gate_in.shape[0]
    outputs = outputs.transpose(0, 2, 1, 3).reshape(length, HV, DV)
    mean_square = lax.optimization_barrier(jnp.mean(outputs * outputs, -1, keepdims=True))
    gate_heads = gate_in.astype(jnp.float32).reshape(length, HV, DV)
    normed = (outputs * lax.rsqrt(mean_square + EPSILON) * head_gain * jax.nn.silu(gate_heads)).reshape(length, HV * DV).astype(jnp.bfloat16)
    mixed = jnp.dot(normed.astype(jnp.float32), out_proj.astype(jnp.float32), preferred_element_type=jnp.float32)
    return (residual_in.astype(jnp.float32) + mixed).astype(jnp.bfloat16)

def post_norm(hidden_state, post_gain):
    widened = hidden_state.astype(jnp.float32)
    return (widened * lax.rsqrt(lax.optimization_barrier(jnp.mean(widened * widened, -1, keepdims=True)) + EPSILON) * post_gain).astype(jnp.bfloat16)

def rank_of(flat_ids, experts):
    onehot = (flat_ids[:, None] == jnp.arange(experts, dtype=jnp.int32)[None, :]).astype(jnp.int32)
    return lax.optimization_barrier(jnp.sum((jnp.cumsum(onehot, 0) - onehot) * onehot, 1))

def reference(queries, key_in, value_in, gate_in, residual_in, log_decay, beta_logit, lengths, head_gain, out_proj, post_gain, expert_in, expert_out, routes, route_gates):
    positions = jnp.arange(PACK_POSITIONS, dtype=jnp.int32)

    def one_pack(pack_args):
        pack_query, pack_keys, pack_values, pack_gates, pack_resid, pack_decay, pack_beta, pack_lengths = pack_args
        segment = segment_of(pack_lengths, positions)
        query_blocks, terms = prepare(pack_query, pack_keys, pack_values, pack_decay, pack_beta, segment, jnp.array(-1, jnp.int32))
        zero_state = jnp.zeros((HV, DK, DV), jnp.float32)
        return finish(query_blocks, terms, zero_state, pack_gates, pack_resid, head_gain, out_proj)
    hidden_state = lax.map(one_pack, (queries, key_in, value_in, gate_in, residual_in, log_decay, beta_logit, lengths))
    blocks = N_DP * N_CTX
    expert_input = post_norm(hidden_state, post_gain).reshape(blocks, TOK_DEV, D)
    flat_ids = routes.reshape(blocks, TOK_DEV * TOPK)

    def block_rank(block_ids):
        return rank_of(block_ids, EXPERTS)
    slot_rank = jax.vmap(block_rank)(flat_ids)

    def fill_block(member):
        block_rows, block_ids, block_ranks = member
        return jnp.zeros((EXPERTS, CAP, D), jnp.bfloat16).at[block_ids, block_ranks].set(jnp.repeat(block_rows, TOPK, axis=0))
    buffers = lax.map(fill_block, (expert_input, flat_ids, slot_rank))

    def run_expert(expert_index):
        routed_rows = lax.dynamic_index_in_dim(buffers, expert_index, 1, keepdims=False).reshape(blocks * CAP, D)
        gate_up = jnp.dot(routed_rows.astype(jnp.float32), lax.dynamic_index_in_dim(expert_in, expert_index, 0, keepdims=False).astype(jnp.float32), preferred_element_type=jnp.float32)
        hidden_units = (jax.nn.silu(gate_up[:, :FF]) * gate_up[:, FF:]).astype(jnp.bfloat16)
        result = jnp.dot(hidden_units.astype(jnp.float32), lax.dynamic_index_in_dim(expert_out, expert_index, 0, keepdims=False).astype(jnp.float32), preferred_element_type=jnp.float32)
        return result.astype(jnp.bfloat16).reshape(blocks, CAP, D)
    results = lax.map(run_expert, jnp.arange(EXPERTS, dtype=jnp.int32))

    def gather_back(member):
        block_index, block_ids, block_ranks, block_gates = member
        picked = results[block_ids, block_index, block_ranks].astype(jnp.float32).reshape(TOK_DEV, TOPK, D)
        return lax.optimization_barrier(jnp.sum(picked * block_gates[:, :, None], 1))
    expert_mix = lax.map(gather_back, (jnp.arange(blocks, dtype=jnp.int32), flat_ids, slot_rank, route_gates.reshape(blocks, TOK_DEV, TOPK)))
    summed = hidden_state.reshape(blocks, TOK_DEV, D).astype(jnp.float32) + expert_mix
    return summed.reshape(PACKS, PACK_POSITIONS, D).astype(jnp.bfloat16)
```

```python
import jax
import jax.numpy as jnp
from jax import lax
from jax.experimental import pallas as pl
from jax.experimental.pallas import tpu as pltpu
from jax.sharding import PartitionSpec as P

D = 2048
DK = 128
DV = 128
FF = 512
TOPK = 10
HK = 8
HV = 16
BLOCK = 64


EPSILON = 1e-06
HIGHEST = lax.Precision.HIGHEST
ROWWISE = lax.Precision.HIGH


def entering(part, axis, combine, identity):
    place = lax.axis_index(axis)
    gathered = jax.tree.map(lambda a: lax.all_gather(a, axis), part)
    state = jax.tree.map(lambda a, e: jnp.zeros_like(a) + jnp.asarray(e, a.dtype), part, identity)

    def one(lap, state):
        return combine(
            state, jax.tree.map(lambda a: lax.dynamic_index_in_dim(a, lap, 0, False), gathered)
        )

    return lax.fori_loop(0, place, one, state)


def unit_heads(matrix, head_count, factor):
    shaped = matrix.astype(jnp.float32).reshape(matrix.shape[0], head_count, -1)
    return shaped * lax.rsqrt(jnp.sum(shaped * shaped, -1, keepdims=True) + EPSILON) * factor


def segment_of(lengths, positions):
    starts = jnp.cumsum(lengths) - lengths
    return jnp.sum((starts[:, None] <= positions[None, :]).astype(jnp.int32), 0) - 1


def block_terms(queries, key_rows, value_rows, beta_gate, decay_log, segment, seg_before):
    length = key_rows.shape[1]
    cumulative = jnp.cumsum(decay_log, axis=-1)
    rows_at = jnp.arange(length)[:, None]
    cols_at = jnp.arange(length)[None, :]
    same_doc = (segment[:, None] == segment[None, :]) & (rows_at >= cols_at)
    log_gap = jnp.minimum(cumulative[:, :, None] - cumulative[:, None, :], 0.0)
    decay_pair = jnp.where(same_doc[None], jnp.exp(log_gap), 0.0)
    from_start = jnp.where((segment == seg_before)[None, :], jnp.exp(cumulative), 0.0)
    to_end = decay_pair[:, -1, :]
    key_inner = jnp.einsum("hcd,hsd->hcs", key_rows, key_rows, precision=ROWWISE)
    lower_part = jnp.where(
        (rows_at > cols_at)[None], beta_gate[:, :, None] * decay_pair * key_inner, 0.0
    )
    system = jnp.eye(length, dtype=jnp.float32)[None] + lower_part
    right_side = jnp.concatenate(
        [beta_gate[:, :, None] * value_rows, (beta_gate * from_start)[:, :, None] * key_rows],
        axis=-1,
    )
    solved = jax.scipy.linalg.solve_triangular(system, right_side, lower=True, unit_diagonal=True)
    value_width = value_rows.shape[-1]
    pseudo = solved[..., :value_width]
    weights = solved[..., value_width:]
    scores = jnp.einsum("hcd,hsd->hcs", queries, key_rows, precision=ROWWISE) * decay_pair
    weighted = key_rows * to_end[:, :, None]
    key_width = key_rows.shape[-1]
    transition = from_start[:, -1][:, None, None] * jnp.eye(key_width, dtype=jnp.float32)[
        None
    ] - jnp.einsum("hcd,hce->hde", weighted, weights, precision=HIGHEST)
    offset = jnp.einsum("hcd,hce->hde", weighted, pseudo, precision=HIGHEST)
    return (pseudo, weights, scores, from_start, transition, offset)


def block_output(queries, pseudo, weights, scores, from_start, carried):
    errors = pseudo - jnp.einsum("hcd,hde->hce", weights, carried, precision=ROWWISE)
    return jnp.einsum(
        "hcd,hde->hce", queries * from_start[:, :, None], carried, precision=ROWWISE
    ) + jnp.einsum("hcs,hse->hce", scores, errors, precision=ROWWISE)


def apply_map(transition, carried):
    return jnp.einsum("hde,hef->hdf", transition, carried, precision=HIGHEST)


def head_blocks(matrix, block_len):
    length, head_count, inner_width = matrix.shape
    return matrix.reshape(length // block_len, block_len, head_count, inner_width).transpose(
        0, 2, 1, 3
    )


def prepare(queries, key_in, value_in, log_decay, beta_logit, segment, seg_before):
    length = queries.shape[0]
    group_size = HV // HK
    query_heads = jnp.repeat(unit_heads(queries, HK, DK ** (-0.5)), group_size, axis=1)
    key_heads = jnp.repeat(unit_heads(key_in, HK, 1.0), group_size, axis=1)
    value_heads = value_in.astype(jnp.float32).reshape(length, HV, DV)
    nblock = length // BLOCK
    beta_gate = jax.nn.sigmoid(beta_logit).reshape(HV, nblock, BLOCK).transpose(1, 0, 2)
    decay_log = log_decay.reshape(HV, nblock, BLOCK).transpose(1, 0, 2)
    seg_blocks = segment.reshape(nblock, BLOCK)
    seg_starts = jnp.concatenate([jnp.reshape(seg_before, (1,)), seg_blocks[:-1, -1]])
    query_blocks = head_blocks(query_heads, BLOCK)
    terms = jax.vmap(block_terms)(
        query_blocks,
        head_blocks(key_heads, BLOCK),
        head_blocks(value_heads, BLOCK),
        beta_gate,
        decay_log,
        seg_blocks,
        seg_starts,
    )
    return (query_blocks, terms)


def finish(query_blocks, terms, start_state, gate_in, residual_in, head_gain, out_proj):
    pseudo, weights, scores, from_start, transition, offset = terms

    def advance(carried, member):
        return (apply_map(member[0], carried) + member[1], carried)

    final_state, block_starts = lax.scan(advance, start_state, (transition, offset))
    outputs = jax.vmap(block_output)(
        query_blocks, pseudo, weights, scores, from_start, block_starts
    )
    length = gate_in.shape[0]
    outputs = outputs.transpose(0, 2, 1, 3).reshape(length, HV, DV)
    mean_square = jnp.mean(outputs * outputs, -1, keepdims=True)
    gate_heads = gate_in.astype(jnp.float32).reshape(length, HV, DV)
    normed = (
        (outputs * lax.rsqrt(mean_square + EPSILON) * head_gain * jax.nn.silu(gate_heads))
        .reshape(length, HV * DV)
        .astype(jnp.bfloat16)
    )
    mixed = jnp.dot(normed, out_proj, preferred_element_type=jnp.float32)
    return (residual_in.astype(jnp.float32) + mixed).astype(jnp.bfloat16)


def post_norm(hidden_state, post_gain):
    widened = hidden_state.astype(jnp.float32)
    return (
        widened * lax.rsqrt(jnp.mean(widened * widened, -1, keepdims=True) + EPSILON) * post_gain
    ).astype(jnp.bfloat16)


def rank_of(flat_ids, experts):
    onehot = (flat_ids[:, None] == jnp.arange(experts, dtype=jnp.int32)[None, :]).astype(jnp.int32)
    return jnp.sum((jnp.cumsum(onehot, 0) - onehot) * onehot, 1)


def expert_apply(routed, expert_in, expert_out):
    gate_up = jnp.einsum("sjcd,jdf->sjcf", routed, expert_in, preferred_element_type=jnp.float32)
    hidden_units = (jax.nn.silu(gate_up[..., :FF]) * gate_up[..., FF:]).astype(jnp.bfloat16)
    return jnp.einsum(
        "sjcf,jfd->sjcd", hidden_units, expert_out, preferred_element_type=jnp.float32
    ).astype(jnp.bfloat16)


def per_device_long(
    queries,
    key_in,
    value_in,
    gate_in,
    residual_in,
    log_decay,
    beta_logit,
    lengths,
    head_gain,
    out_proj,
    post_gain,
    expert_in,
    expert_out,
    routes,
    route_gates,
):
    tokens_dev = queries.shape[1]
    ctx_index = lax.axis_index("ctx")
    positions = ctx_index * tokens_dev + jnp.arange(tokens_dev, dtype=jnp.int32)
    segment = segment_of(lengths[0], positions)
    previous = segment_of(lengths[0], jnp.reshape(positions[0] - 1, (1,)))[0]
    seg_before = jnp.where(ctx_index > 0, previous, -1)
    query_blocks, terms = prepare(
        queries[0], key_in[0], value_in[0], log_decay[0], beta_logit[0], segment, seg_before
    )
    eye_maps = jnp.broadcast_to(jnp.eye(DK, dtype=jnp.float32), (HV, DK, DK))
    zero_offset = jnp.zeros((HV, DK, DV), jnp.float32)

    def compose(carry_pair, member):
        return (
            (apply_map(member[0], carry_pair[0]), apply_map(member[0], carry_pair[1]) + member[1]),
            None,
        )

    device_pair, unused = lax.scan(compose, (eye_maps, zero_offset), (terms[4], terms[5]))

    def combine(earlier, later):
        return (apply_map(later[0], earlier[0]), apply_map(later[0], earlier[1]) + later[1])

    prefix_map, prefix_offset = entering(
        (device_pair[0], device_pair[1]), "ctx", combine, (eye_maps, zero_offset)
    )
    hidden_state = finish(
        query_blocks, terms, prefix_offset, gate_in[0], residual_in[0], head_gain, out_proj
    )
    expert_input = post_norm(hidden_state, post_gain)
    local_experts = expert_in.shape[0]
    device_count = lax.axis_size("dp") * lax.axis_size("ctx")
    experts_all = local_experts * device_count
    capacity = tokens_dev * TOPK * 6 // (5 * experts_all)
    flat_ids = routes[0].reshape(-1)
    slot_rank = rank_of(flat_ids, experts_all)
    outbound = (
        jnp.zeros((experts_all, capacity, D), jnp.bfloat16)
        .at[flat_ids, slot_rank]
        .set(jnp.repeat(expert_input, TOPK, axis=0))
    )
    outbound = outbound.reshape(device_count, local_experts, capacity, D)
    computed = expert_apply(
        lax.all_to_all(outbound, ("dp", "ctx"), split_axis=0, concat_axis=0, tiled=True),
        expert_in,
        expert_out,
    )
    returned = lax.all_to_all(computed, ("dp", "ctx"), split_axis=0, concat_axis=0, tiled=True)
    back_rows = returned.reshape(experts_all, capacity, D)[flat_ids, slot_rank]
    expert_mix = jnp.sum(
        back_rows.astype(jnp.float32).reshape(tokens_dev, TOPK, D) * route_gates[0][:, :, None], 1
    )
    summed = hidden_state.astype(jnp.float32) + expert_mix
    return summed.astype(jnp.bfloat16)[None]


TILE = 128
SCAL = 128
BF = jnp.bfloat16
F32 = jnp.float32


def mm(a, b):
    return jnp.dot(a, b, preferred_element_type=F32)


def mm_nt(a, b):
    return lax.dot_general(a, b, (((1,), (1,)), ((), ())), preferred_element_type=F32)


def halves(a):
    high = a.astype(BF)
    return high, (a - high.astype(F32)).astype(BF)


def dot3(a, b):
    ah, al = a
    bh, bl = b
    return mm(ah, bh) + (mm(ah, bl) + mm(al, bh))


def mixer_kernel(lengths_ref, x_ref, gain_ref, out_ref, pseudo, weights, scores, keyed, ends):
    total = x_ref.shape[0]
    tiles = total // TILE
    group = HV // HK
    rows = lax.broadcasted_iota(jnp.int32, (TILE, TILE), 0)
    cols = lax.broadcasted_iota(jnp.int32, (TILE, TILE), 1)
    eye = (rows == cols).astype(F32)
    tri = (rows >= cols).astype(BF)
    starts = []
    at = jnp.int32(0)
    for j in range(lengths_ref.shape[1]):
        starts.append(at)
        at = at + lengths_ref[0, j]

    def segment(pos):
        seg = jnp.zeros(pos.shape, jnp.int32)
        for start in starts:
            seg = seg + (start <= pos).astype(jnp.int32)
        return seg

    def terms_of(tile):
        base = pl.multiple_of(tile * TILE, TILE)
        q = x_ref[pl.ds(base, TILE), 0:DK]
        k = x_ref[pl.ds(base, TILE), DK : 2 * DK]
        sc = x_ref[pl.ds(base, TILE), 2 * DK + group * DV : 2 * DK + group * DV + SCAL]
        cum = mm(tri, sc)
        qf = q.astype(F32)
        kf = k.astype(F32)
        rq = lax.rsqrt(jnp.sum(qf * qf, -1, keepdims=True) + EPSILON) * DK ** (-0.5)
        rk = lax.rsqrt(jnp.sum(kf * kf, -1, keepdims=True) + EPSILON)
        scf = sc.astype(F32)
        seg_c = segment(base + rows)
        seg_r = segment(base + cols)
        seg_b = segment(jnp.full((TILE, 1), base - 1, jnp.int32))
        causal = (seg_c == seg_r) & (rows >= cols)
        open_c = (seg_c[:, :1] == seg_b) & (base > 0)
        g_c, beta_c, from_c = [], [], []
        for h in range(group):
            g = cum[:, h : h + 1] + cum[:, group + h : group + h + 1]
            b = (
                scf[:, 2 * group + h : 2 * group + h + 1]
                + scf[:, 3 * group + h : 3 * group + h + 1]
            )
            g_c.append(g)
            beta_c.append(b)
            from_c.append(jnp.where(open_c, jnp.exp(g), 0.0))
        packed = jnp.zeros((TILE, TILE), F32)
        for n, col in enumerate(g_c + beta_c + from_c + [rk]):
            packed = jnp.where(cols == n, col, packed)
        flat = packed.T
        rk_r = flat[3 * group : 3 * group + 1, :]
        kk = mm_nt(k, k) * rk * rk_r
        qk = mm_nt(q, k) * rq * rk_r
        per_head = []
        for h in range(group):
            g_r = flat[h : h + 1, :]
            beta_r = flat[group + h : group + h + 1, :]
            from_r = flat[2 * group + h : 2 * group + h + 1, :]
            pair = jnp.where(causal, jnp.exp(jnp.minimum(g_c[h] - g_r, 0.0)), 0.0)
            lower = jnp.where(rows > cols, beta_c[h] * pair * kk, 0.0)
            last = jnp.where(
                (seg_c[TILE - 1 :, :1] == seg_c[:, :1]),
                jnp.exp(jnp.minimum(g_c[h][TILE - 1 :, :] - g_c[h], 0.0)),
                0.0,
            )
            per_head.append(
                dict(
                    tile=tile,
                    h=h,
                    base=base,
                    lower=lower,
                    score=qk * pair,
                    beta_r=beta_r,
                    scale_r=beta_r * from_r * rk_r,
                    k=k,
                    to_end=last * rk,
                    read=from_c[h] * rq,
                    from_end=from_c[h][TILE - 1 :, :],
                )
            )
        return per_head

    def build(step, carry):
        work = []
        for u in range(2):
            work += terms_of(step * 2 + u)
        near = ((rows ^ cols) == 1) & (rows > cols)
        inverse = [eye - jnp.where(near, w["lower"], 0.0) for w in work]
        level = 1
        while (1 << level) < TILE:
            mask = (((rows >> level) ^ (cols >> level)) == 1) & (rows > cols)
            parts = [halves(x) for x in inverse]
            links = [halves(jnp.where(mask, w["lower"], 0.0)) for w in work]
            first = [halves(dot3(x, c)) for x, c in zip(parts, links)]
            inverse = [x - dot3(f, p) for x, f, p in zip(inverse, first, parts)]
            level += 1
        for w, x in zip(work, inverse):
            slot = w["tile"] * group + w["h"]
            v = x_ref[
                pl.ds(w["base"], TILE), 2 * DK + w["h"] * DV : 2 * DK + (w["h"] + 1) * DV
            ]
            xh, xl = halves(x * w["beta_r"])
            pseudo[slot] = mm(xh, v) + mm(xl, v)
            wh, wl = halves(x * w["scale_r"])
            weights[slot] = mm(wh, w["k"]) + mm(wl, w["k"])
            scores[slot] = w["score"]
            keyed[slot] = jnp.where(cols == 0, w["to_end"], jnp.where(cols == 1, w["read"], 0.0))
            ends[slot] = jnp.broadcast_to(w["from_end"], (8, TILE))
        return carry

    lax.fori_loop(0, tiles // 2, build, 0)

    def advance(tile, states):
        base = pl.multiple_of(tile * TILE, TILE)
        q = x_ref[pl.ds(base, TILE), 0:DK]
        k = x_ref[pl.ds(base, TILE), DK : 2 * DK]
        following = []
        for h in range(group):
            slot = tile * group + h
            state = states[h]
            sh, sl = halves(state)
            error = pseudo[slot] - dot3(halves(weights[slot]), (sh, sl))
            scalars = keyed[slot]
            eh, el = halves(error * scalars[:, 0:1])
            grown = lax.dot_general(
                k, eh, (((0,), (0,)), ((), ())), preferred_element_type=F32
            ) + lax.dot_general(k, el, (((0,), (0,)), ((), ())), preferred_element_type=F32)
            following.append(ends[slot][0:1, :] * state + grown)
            raw = (mm(q, sh) + mm(q, sl)) * scalars[:, 1:2] + dot3(
                halves(scores[slot]), halves(error)
            )
            mean = jnp.mean(raw * raw, -1, keepdims=True)
            out_ref[pl.ds(base, TILE), h * DV : (h + 1) * DV] = (
                raw * lax.rsqrt(mean + EPSILON) * gain_ref[...]
            ).astype(BF)
        return tuple(following)

    lax.fori_loop(
        0, tiles, advance, tuple(jnp.zeros((DK, DV), F32) for h in range(group))
    )


def mixer(lengths, rows, head_gain):
    total = rows.shape[0]
    group = HV // HK
    slots = total // TILE * group
    vmem = pl.BlockSpec(memory_space=pltpu.VMEM)
    return pl.pallas_call(
        mixer_kernel,
        out_shape=jax.ShapeDtypeStruct((total, group * DV), BF),
        in_specs=[pl.BlockSpec(memory_space=pltpu.SMEM), vmem, vmem],
        out_specs=vmem,
        scratch_shapes=[
            pltpu.VMEM((slots, TILE, DV), F32),
            pltpu.VMEM((slots, TILE, DK), F32),
            pltpu.VMEM((slots, TILE, TILE), F32),
            pltpu.VMEM((slots, TILE, TILE), F32),
            pltpu.VMEM((slots, 8, TILE), F32),
        ],
        compiler_params=pltpu.CompilerParams(vmem_limit_bytes=40 * 1024 * 1024),
    )(lengths, rows, head_gain.reshape(1, DV))


def two_parts(a):
    high = lax.reduce_precision(a, 8, 7)
    return high.astype(BF), (a - high).astype(BF)


def slot_table(gate_rows, capacity):
    named = gate_rows > 0.0
    tokens = gate_rows.shape[-1]
    before = (
        jnp.arange(tokens, dtype=jnp.int32)[:, None] < jnp.arange(tokens, dtype=jnp.int32)[None, :]
    ).astype(BF)
    rank = jnp.einsum("...t,tu->...u", named.astype(BF), before, preferred_element_type=F32)
    slot = jnp.arange(capacity, dtype=jnp.int32).astype(F32)
    return named[..., None, :] & (rank[..., None, :] == slot[:, None])


def per_device(
    queries,
    key_in,
    value_in,
    gate_in,
    residual_in,
    log_decay,
    beta_logit,
    lengths,
    head_gain,
    out_proj,
    post_gain,
    expert_in,
    expert_out,
    routes,
    route_gates,
):
    tokens = queries.shape[1]
    n_ctx = lax.axis_size("ctx")
    n_dp = lax.axis_size("dp")
    local = expert_in.shape[0]
    devices = n_ctx * n_dp
    experts = local * devices
    capacity = tokens * TOPK * 6 // (5 * experts)
    group = HV // HK
    my_dp = lax.axis_index("dp")
    my_ctx = lax.axis_index("ctx")

    ids = jnp.arange(experts, dtype=jnp.int32)[:, None]
    gate_table = jnp.zeros((experts, tokens), F32)
    for k in range(TOPK):
        gate_table = gate_table + jnp.where(
            routes[0, :, k][None, :] == ids, route_gates[0, :, k][None, :], 0.0
        )
    all_gates = lax.all_gather(gate_table, ("dp", "ctx"))

    beta = jax.nn.sigmoid(beta_logit[0])
    dh, dl = two_parts(log_decay[0])
    bh, bl = two_parts(beta)
    scal = jnp.stack([dh, dl, bh, bl]).reshape(4, n_ctx, group, tokens)
    scal = scal.transpose(1, 3, 0, 2).reshape(n_ctx, tokens, 4 * group)
    scal = jnp.pad(scal, ((0, 0), (0, 0), (0, SCAL - 4 * group)))

    def by_head(a):
        return a[0].reshape(tokens, n_ctx, -1).transpose(1, 0, 2)

    sent = jnp.concatenate([by_head(queries), by_head(key_in), by_head(value_in), scal], -1)
    heads = lax.all_to_all(sent, "ctx", split_axis=0, concat_axis=0, tiled=True)
    mixed = mixer(lengths, heads.reshape(n_ctx * tokens, -1), head_gain)
    mine = lax.all_to_all(
        mixed.reshape(n_ctx, tokens, group * DV), "ctx", split_axis=0, concat_axis=0, tiled=True
    )
    unit = mine.transpose(1, 0, 2).reshape(tokens, HV * DV)
    normed = (unit.astype(F32) * jax.nn.silu(gate_in[0].astype(F32))).astype(BF)
    projected = jnp.dot(normed, out_proj, preferred_element_type=F32)
    hidden_state = (residual_in[0].astype(F32) + projected).astype(BF)
    expert_input = post_norm(hidden_state, post_gain)

    column = lax.all_gather(expert_input, "dp")
    features = lax.all_gather(column, "ctx")
    features = features.reshape(devices, tokens, D)
    by_dev = all_gates.reshape(n_dp, n_ctx, n_dp, n_ctx, local, tokens)
    my_gates = lax.dynamic_index_in_dim(
        lax.dynamic_index_in_dim(by_dev, my_dp, 2, False), my_ctx, 2, False
    )
    my_gates = my_gates.transpose(1, 0, 2, 3).reshape(devices, local, tokens)
    pick = slot_table(my_gates, capacity).astype(BF).transpose(1, 0, 2, 3)
    routed = jnp.einsum("jsct,std->jscd", pick, features, preferred_element_type=F32)
    routed = routed.astype(BF).reshape(local, devices * capacity, D)
    gate_up = jnp.einsum("jrd,jdf->jrf", routed, expert_in, preferred_element_type=F32)
    hidden_units = (jax.nn.silu(gate_up[..., :FF]) * gate_up[..., FF:]).astype(BF)
    result = jnp.einsum("jrf,jfd->jrd", hidden_units, expert_out, preferred_element_type=F32)
    result = result.astype(BF).reshape(local, n_ctx, n_dp, capacity, D).transpose(1, 2, 0, 3, 4)
    returned = lax.all_to_all(result, "ctx", split_axis=0, concat_axis=0, tiled=True)

    plane = lax.dynamic_index_in_dim(by_dev, my_ctx, 1, False)
    plane = lax.dynamic_index_in_dim(plane, my_dp, 1, False)
    table = slot_table(plane, capacity)
    weight = jnp.where(table, plane[..., None, :], 0.0).astype(BF)
    partial = jnp.einsum("pejct,epjcd->ptd", weight, returned, preferred_element_type=F32)
    summed = lax.all_to_all(
        partial.astype(BF), "dp", split_axis=0, concat_axis=0, tiled=True
    )
    total = hidden_state.astype(F32) + jnp.sum(summed.astype(F32), 0)
    return total.astype(BF)[None]


def solution(mesh):
    in_specs = (
        P("dp", "ctx", None),
        P("dp", "ctx", None),
        P("dp", "ctx", None),
        P("dp", "ctx", None),
        P("dp", "ctx", None),
        P("dp", None, "ctx"),
        P("dp", None, "ctx"),
        P("dp", None),
        P(),
        P(),
        P(),
        P(("dp", "ctx"), None, None),
        P(("dp", "ctx"), None, None),
        P("dp", "ctx", None),
        P("dp", "ctx", None),
    )
    out_specs = P("dp", "ctx", None)
    by_heads = mesh.shape["ctx"] == HK
    return jax.shard_map(
        per_device if by_heads else per_device_long, mesh=mesh, in_specs=in_specs, out_specs=out_specs, check_vma=False
    )
```

```python
import functools

import jax
import jax.numpy as jnp
from jax import lax
from jax.experimental import pallas as pl
from jax.experimental.pallas import tpu as pltpu
from jax.sharding import PartitionSpec as P

D = 2048
DK = 128
DV = 128
FF = 512
TOPK = 10
HK = 8
HV = 16
BLOCK = 64


EPSILON = 1e-06
HIGHEST = lax.Precision.HIGHEST
ROWWISE = lax.Precision.HIGH


def entering(part, axis, combine, identity):
    place = lax.axis_index(axis)
    gathered = jax.tree.map(lambda a: lax.all_gather(a, axis), part)
    state = jax.tree.map(lambda a, e: jnp.zeros_like(a) + jnp.asarray(e, a.dtype), part, identity)

    def one(lap, state):
        return combine(
            state, jax.tree.map(lambda a: lax.dynamic_index_in_dim(a, lap, 0, False), gathered)
        )

    return lax.fori_loop(0, place, one, state)


def unit_heads(matrix, head_count, factor):
    shaped = matrix.astype(jnp.float32).reshape(matrix.shape[0], head_count, -1)
    return shaped * lax.rsqrt(jnp.sum(shaped * shaped, -1, keepdims=True) + EPSILON) * factor


def segment_of(lengths, positions):
    starts = jnp.cumsum(lengths) - lengths
    return jnp.sum((starts[:, None] <= positions[None, :]).astype(jnp.int32), 0) - 1


def block_terms(queries, key_rows, value_rows, beta_gate, decay_log, segment, seg_before):
    length = key_rows.shape[1]
    cumulative = jnp.cumsum(decay_log, axis=-1)
    rows_at = jnp.arange(length)[:, None]
    cols_at = jnp.arange(length)[None, :]
    same_doc = (segment[:, None] == segment[None, :]) & (rows_at >= cols_at)
    log_gap = jnp.minimum(cumulative[:, :, None] - cumulative[:, None, :], 0.0)
    decay_pair = jnp.where(same_doc[None], jnp.exp(log_gap), 0.0)
    from_start = jnp.where((segment == seg_before)[None, :], jnp.exp(cumulative), 0.0)
    to_end = decay_pair[:, -1, :]
    key_inner = jnp.einsum("hcd,hsd->hcs", key_rows, key_rows, precision=ROWWISE)
    lower_part = jnp.where(
        (rows_at > cols_at)[None], beta_gate[:, :, None] * decay_pair * key_inner, 0.0
    )
    system = jnp.eye(length, dtype=jnp.float32)[None] + lower_part
    right_side = jnp.concatenate(
        [beta_gate[:, :, None] * value_rows, (beta_gate * from_start)[:, :, None] * key_rows],
        axis=-1,
    )
    solved = jax.scipy.linalg.solve_triangular(system, right_side, lower=True, unit_diagonal=True)
    value_width = value_rows.shape[-1]
    pseudo = solved[..., :value_width]
    weights = solved[..., value_width:]
    scores = jnp.einsum("hcd,hsd->hcs", queries, key_rows, precision=ROWWISE) * decay_pair
    weighted = key_rows * to_end[:, :, None]
    key_width = key_rows.shape[-1]
    transition = from_start[:, -1][:, None, None] * jnp.eye(key_width, dtype=jnp.float32)[
        None
    ] - jnp.einsum("hcd,hce->hde", weighted, weights, precision=HIGHEST)
    offset = jnp.einsum("hcd,hce->hde", weighted, pseudo, precision=HIGHEST)
    return (pseudo, weights, scores, from_start, transition, offset)


def block_output(queries, pseudo, weights, scores, from_start, carried):
    errors = pseudo - jnp.einsum("hcd,hde->hce", weights, carried, precision=ROWWISE)
    return jnp.einsum(
        "hcd,hde->hce", queries * from_start[:, :, None], carried, precision=ROWWISE
    ) + jnp.einsum("hcs,hse->hce", scores, errors, precision=ROWWISE)


def apply_map(transition, carried):
    return jnp.einsum("hde,hef->hdf", transition, carried, precision=HIGHEST)


def head_blocks(matrix, block_len):
    length, head_count, inner_width = matrix.shape
    return matrix.reshape(length // block_len, block_len, head_count, inner_width).transpose(
        0, 2, 1, 3
    )


def prepare(queries, key_in, value_in, log_decay, beta_logit, segment, seg_before):
    length = queries.shape[0]
    group_size = HV // HK
    query_heads = jnp.repeat(unit_heads(queries, HK, DK ** (-0.5)), group_size, axis=1)
    key_heads = jnp.repeat(unit_heads(key_in, HK, 1.0), group_size, axis=1)
    value_heads = value_in.astype(jnp.float32).reshape(length, HV, DV)
    nblock = length // BLOCK
    beta_gate = jax.nn.sigmoid(beta_logit).reshape(HV, nblock, BLOCK).transpose(1, 0, 2)
    decay_log = log_decay.reshape(HV, nblock, BLOCK).transpose(1, 0, 2)
    seg_blocks = segment.reshape(nblock, BLOCK)
    seg_starts = jnp.concatenate([jnp.reshape(seg_before, (1,)), seg_blocks[:-1, -1]])
    query_blocks = head_blocks(query_heads, BLOCK)
    terms = jax.vmap(block_terms)(
        query_blocks,
        head_blocks(key_heads, BLOCK),
        head_blocks(value_heads, BLOCK),
        beta_gate,
        decay_log,
        seg_blocks,
        seg_starts,
    )
    return (query_blocks, terms)


def finish(query_blocks, terms, start_state, gate_in, residual_in, head_gain, out_proj):
    pseudo, weights, scores, from_start, transition, offset = terms

    def advance(carried, member):
        return (apply_map(member[0], carried) + member[1], carried)

    final_state, block_starts = lax.scan(advance, start_state, (transition, offset))
    outputs = jax.vmap(block_output)(
        query_blocks, pseudo, weights, scores, from_start, block_starts
    )
    length = gate_in.shape[0]
    outputs = outputs.transpose(0, 2, 1, 3).reshape(length, HV, DV)
    mean_square = jnp.mean(outputs * outputs, -1, keepdims=True)
    gate_heads = gate_in.astype(jnp.float32).reshape(length, HV, DV)
    normed = (
        (outputs * lax.rsqrt(mean_square + EPSILON) * head_gain * jax.nn.silu(gate_heads))
        .reshape(length, HV * DV)
        .astype(jnp.bfloat16)
    )
    mixed = jnp.dot(normed, out_proj, preferred_element_type=jnp.float32)
    return (residual_in.astype(jnp.float32) + mixed).astype(jnp.bfloat16)


def post_norm(hidden_state, post_gain):
    widened = hidden_state.astype(jnp.float32)
    return (
        widened * lax.rsqrt(jnp.mean(widened * widened, -1, keepdims=True) + EPSILON) * post_gain
    ).astype(jnp.bfloat16)


def rank_of(flat_ids, experts):
    onehot = (flat_ids[:, None] == jnp.arange(experts, dtype=jnp.int32)[None, :]).astype(jnp.int32)
    return jnp.sum((jnp.cumsum(onehot, 0) - onehot) * onehot, 1)


def expert_apply(routed, expert_in, expert_out):
    gate_up = jnp.einsum("sjcd,jdf->sjcf", routed, expert_in, preferred_element_type=jnp.float32)
    hidden_units = (jax.nn.silu(gate_up[..., :FF]) * gate_up[..., FF:]).astype(jnp.bfloat16)
    return jnp.einsum(
        "sjcf,jfd->sjcd", hidden_units, expert_out, preferred_element_type=jnp.float32
    ).astype(jnp.bfloat16)


def per_device_long(
    queries,
    key_in,
    value_in,
    gate_in,
    residual_in,
    log_decay,
    beta_logit,
    lengths,
    head_gain,
    out_proj,
    post_gain,
    expert_in,
    expert_out,
    routes,
    route_gates,
):
    tokens_dev = queries.shape[1]
    ctx_index = lax.axis_index("ctx")
    positions = ctx_index * tokens_dev + jnp.arange(tokens_dev, dtype=jnp.int32)
    segment = segment_of(lengths[0], positions)
    previous = segment_of(lengths[0], jnp.reshape(positions[0] - 1, (1,)))[0]
    seg_before = jnp.where(ctx_index > 0, previous, -1)
    query_blocks, terms = prepare(
        queries[0], key_in[0], value_in[0], log_decay[0], beta_logit[0], segment, seg_before
    )
    eye_maps = jnp.broadcast_to(jnp.eye(DK, dtype=jnp.float32), (HV, DK, DK))
    zero_offset = jnp.zeros((HV, DK, DV), jnp.float32)

    def compose(carry_pair, member):
        return (
            (apply_map(member[0], carry_pair[0]), apply_map(member[0], carry_pair[1]) + member[1]),
            None,
        )

    device_pair, unused = lax.scan(compose, (eye_maps, zero_offset), (terms[4], terms[5]))

    def combine(earlier, later):
        return (apply_map(later[0], earlier[0]), apply_map(later[0], earlier[1]) + later[1])

    prefix_map, prefix_offset = entering(
        (device_pair[0], device_pair[1]), "ctx", combine, (eye_maps, zero_offset)
    )
    hidden_state = finish(
        query_blocks, terms, prefix_offset, gate_in[0], residual_in[0], head_gain, out_proj
    )
    expert_input = post_norm(hidden_state, post_gain)
    local_experts = expert_in.shape[0]
    device_count = lax.axis_size("dp") * lax.axis_size("ctx")
    experts_all = local_experts * device_count
    capacity = tokens_dev * TOPK * 6 // (5 * experts_all)
    flat_ids = routes[0].reshape(-1)
    slot_rank = rank_of(flat_ids, experts_all)
    outbound = (
        jnp.zeros((experts_all, capacity, D), jnp.bfloat16)
        .at[flat_ids, slot_rank]
        .set(jnp.repeat(expert_input, TOPK, axis=0))
    )
    outbound = outbound.reshape(device_count, local_experts, capacity, D)
    computed = expert_apply(
        lax.all_to_all(outbound, ("dp", "ctx"), split_axis=0, concat_axis=0, tiled=True),
        expert_in,
        expert_out,
    )
    returned = lax.all_to_all(computed, ("dp", "ctx"), split_axis=0, concat_axis=0, tiled=True)
    back_rows = returned.reshape(experts_all, capacity, D)[flat_ids, slot_rank]
    expert_mix = jnp.sum(
        back_rows.astype(jnp.float32).reshape(tokens_dev, TOPK, D) * route_gates[0][:, :, None], 1
    )
    summed = hidden_state.astype(jnp.float32) + expert_mix
    return summed.astype(jnp.bfloat16)[None]


TILE = 128
SCAL = 128
BF = jnp.bfloat16
F32 = jnp.float32


def mm(a, b):
    return jnp.dot(a, b, preferred_element_type=F32)


def mm_nt(a, b):
    return lax.dot_general(a, b, (((1,), (1,)), ((), ())), preferred_element_type=F32)


def halves(a):
    high = a.astype(BF)
    return high, (a - high.astype(F32)).astype(BF)


def dot3(a, b):
    ah, al = a
    bh, bl = b
    return mm(ah, bh) + (mm(ah, bl) + mm(al, bh))


def mixer_kernel(lengths_ref, x_ref, gain_ref, out_ref, pseudo, weights, scores, keyed, ends):
    total = x_ref.shape[0]
    tiles = total // TILE
    group = HV // HK
    rows = lax.broadcasted_iota(jnp.int32, (TILE, TILE), 0)
    cols = lax.broadcasted_iota(jnp.int32, (TILE, TILE), 1)
    eye = (rows == cols).astype(F32)
    tri = (rows >= cols).astype(BF)
    starts = []
    at = jnp.int32(0)
    for j in range(lengths_ref.shape[1]):
        starts.append(at)
        at = at + lengths_ref[0, j]

    def segment(pos):
        seg = jnp.zeros(pos.shape, jnp.int32)
        for start in starts:
            seg = seg + (start <= pos).astype(jnp.int32)
        return seg

    def terms_of(tile):
        base = pl.multiple_of(tile * TILE, TILE)
        q = x_ref[pl.ds(base, TILE), 0:DK]
        k = x_ref[pl.ds(base, TILE), DK : 2 * DK]
        sc = x_ref[pl.ds(base, TILE), 2 * DK + group * DV : 2 * DK + group * DV + SCAL]
        cum = mm(tri, sc)
        qf = q.astype(F32)
        kf = k.astype(F32)
        rq = lax.rsqrt(jnp.sum(qf * qf, -1, keepdims=True) + EPSILON) * DK ** (-0.5)
        rk = lax.rsqrt(jnp.sum(kf * kf, -1, keepdims=True) + EPSILON)
        scf = sc.astype(F32)
        seg_c = segment(base + rows)
        seg_r = segment(base + cols)
        seg_b = segment(jnp.full((TILE, 1), base - 1, jnp.int32))
        causal = (seg_c == seg_r) & (rows >= cols)
        open_c = (seg_c[:, :1] == seg_b) & (base > 0)
        g_c, beta_c, from_c = [], [], []
        for h in range(group):
            g = cum[:, h : h + 1] + cum[:, group + h : group + h + 1]
            b = (
                scf[:, 2 * group + h : 2 * group + h + 1]
                + scf[:, 3 * group + h : 3 * group + h + 1]
            )
            g_c.append(g)
            beta_c.append(b)
            from_c.append(jnp.where(open_c, jnp.exp(g), 0.0))
        packed = jnp.zeros((TILE, TILE), F32)
        for n, col in enumerate(g_c + beta_c + from_c + [rk]):
            packed = jnp.where(cols == n, col, packed)
        flat = packed.T
        rk_r = flat[3 * group : 3 * group + 1, :]
        kk = mm_nt(k, k) * rk * rk_r
        qk = mm_nt(q, k) * rq * rk_r
        per_head = []
        for h in range(group):
            g_r = flat[h : h + 1, :]
            beta_r = flat[group + h : group + h + 1, :]
            from_r = flat[2 * group + h : 2 * group + h + 1, :]
            pair = jnp.where(causal, jnp.exp(jnp.minimum(g_c[h] - g_r, 0.0)), 0.0)
            lower = jnp.where(rows > cols, beta_c[h] * pair * kk, 0.0)
            last = jnp.where(
                (seg_c[TILE - 1 :, :1] == seg_c[:, :1]),
                jnp.exp(jnp.minimum(g_c[h][TILE - 1 :, :] - g_c[h], 0.0)),
                0.0,
            )
            per_head.append(
                dict(
                    tile=tile,
                    h=h,
                    base=base,
                    lower=lower,
                    score=qk * pair,
                    beta_r=beta_r,
                    scale_r=beta_r * from_r * rk_r,
                    k=k,
                    to_end=last * rk,
                    read=from_c[h] * rq,
                    from_end=from_c[h][TILE - 1 :, :],
                )
            )
        return per_head

    def build(step, carry):
        work = []
        for u in range(2):
            work += terms_of(step * 2 + u)
        near = ((rows ^ cols) == 1) & (rows > cols)
        inverse = [eye - jnp.where(near, w["lower"], 0.0) for w in work]
        level = 1
        while (1 << level) < TILE:
            mask = (((rows >> level) ^ (cols >> level)) == 1) & (rows > cols)
            parts = [halves(x) for x in inverse]
            links = [halves(jnp.where(mask, w["lower"], 0.0)) for w in work]
            first = [halves(dot3(x, c)) for x, c in zip(parts, links)]
            inverse = [x - dot3(f, p) for x, f, p in zip(inverse, first, parts)]
            level += 1
        for w, x in zip(work, inverse):
            slot = w["tile"] * group + w["h"]
            v = x_ref[
                pl.ds(w["base"], TILE), 2 * DK + w["h"] * DV : 2 * DK + (w["h"] + 1) * DV
            ]
            xh, xl = halves(x * w["beta_r"])
            pseudo[slot] = mm(xh, v) + mm(xl, v)
            wh, wl = halves(x * w["scale_r"])
            weights[slot] = mm(wh, w["k"]) + mm(wl, w["k"])
            scores[slot] = w["score"]
            keyed[slot] = jnp.where(cols == 0, w["to_end"], jnp.where(cols == 1, w["read"], 0.0))
            ends[slot] = jnp.broadcast_to(w["from_end"], (8, TILE))
        return carry

    lax.fori_loop(0, tiles // 2, build, 0)

    def advance(tile, states):
        base = pl.multiple_of(tile * TILE, TILE)
        q = x_ref[pl.ds(base, TILE), 0:DK]
        k = x_ref[pl.ds(base, TILE), DK : 2 * DK]
        following = []
        for h in range(group):
            slot = tile * group + h
            state = states[h]
            sh, sl = halves(state)
            error = pseudo[slot] - dot3(halves(weights[slot]), (sh, sl))
            scalars = keyed[slot]
            eh, el = halves(error * scalars[:, 0:1])
            grown = lax.dot_general(
                k, eh, (((0,), (0,)), ((), ())), preferred_element_type=F32
            ) + lax.dot_general(k, el, (((0,), (0,)), ((), ())), preferred_element_type=F32)
            following.append(ends[slot][0:1, :] * state + grown)
            raw = (mm(q, sh) + mm(q, sl)) * scalars[:, 1:2] + dot3(
                halves(scores[slot]), halves(error)
            )
            mean = jnp.mean(raw * raw, -1, keepdims=True)
            out_ref[pl.ds(base, TILE), h * DV : (h + 1) * DV] = (
                raw * lax.rsqrt(mean + EPSILON) * gain_ref[...]
            ).astype(BF)
        return tuple(following)

    lax.fori_loop(
        0, tiles, advance, tuple(jnp.zeros((DK, DV), F32) for h in range(group))
    )


def mixer(lengths, rows, head_gain):
    total = rows.shape[0]
    group = HV // HK
    slots = total // TILE * group
    vmem = pl.BlockSpec(memory_space=pltpu.VMEM)
    return pl.pallas_call(
        mixer_kernel,
        out_shape=jax.ShapeDtypeStruct((total, group * DV), BF),
        in_specs=[pl.BlockSpec(memory_space=pltpu.SMEM), vmem, vmem],
        out_specs=vmem,
        scratch_shapes=[
            pltpu.VMEM((slots, TILE, DV), F32),
            pltpu.VMEM((slots, TILE, DK), F32),
            pltpu.VMEM((slots, TILE, TILE), F32),
            pltpu.VMEM((slots, TILE, TILE), F32),
            pltpu.VMEM((slots, 8, TILE), F32),
        ],
        compiler_params=pltpu.CompilerParams(vmem_limit_bytes=40 * 1024 * 1024),
    )(lengths, rows, head_gain.reshape(1, DV))


def moe_kernel(
    n_dp, x_ref, hidden_ref, pick_ref, weight_ref, in_hbm, out_hbm, o_ref,
    feat, w_in, w_out, routed, units, sent, got, part, summed,
    load_sem, z_send, z_recv, d_send, d_recv, r_send, r_recv, p_send, p_recv,
):
    z = lax.axis_index("dp")
    me = lax.axis_index("ctx")
    tokens = x_ref.shape[0]
    half = tokens // 2
    rows = sent.shape[2]
    cap = rows // 2
    core, along_x, along_y = me % 2, (me // 2) % 2, me // 4

    def beside(rel):
        c = 1 - core if rel % 2 else core
        x = 1 - along_x if (rel // 2) % 2 else along_x
        y = 1 - along_y if rel // 4 else along_y
        return (z, (y * 2 + x) * 2 + c)

    def above(s):
        return (lax.rem(z + s, n_dp), me)

    def below(s):
        return (lax.rem(z - s + n_dp, n_dp), me)

    loads = [
        pltpu.make_async_copy(in_hbm, w_in, load_sem.at[0]),
        pltpu.make_async_copy(out_hbm, w_out, load_sem.at[1]),
    ]
    for copy in loads:
        copy.start()
    barrier = pltpu.get_barrier_semaphore()
    peers = [above(s) for s in range(1, n_dp)] + [beside(rel) for rel in range(1, 8)]
    for peer in peers:
        pl.semaphore_signal(barrier, inc=1, device_id=peer, device_id_type=pl.DeviceIdType.MESH)
    pl.semaphore_wait(barrier, len(peers))

    started = []

    def push(src, dst, send, recv, peer):
        copy = pltpu.make_async_remote_copy(
            src_ref=src, dst_ref=dst, send_sem=send, recv_sem=recv,
            device_id=peer, device_id_type=pl.DeviceIdType.MESH,
        )
        copy.start()
        started.append(copy)

    def arrived(dst, send, recv, peer):
        pltpu.make_async_remote_copy(
            src_ref=dst, dst_ref=dst, send_sem=send, recv_sem=recv,
            device_id=peer, device_id_type=pl.DeviceIdType.MESH,
        ).wait_recv()

    def spread(s):
        mine = feat.at[s, 0]
        push(mine, feat.at[s, 2], d_send.at[s, 0], d_recv.at[s, 0], beside(2))
        push(mine, feat.at[s, 4], d_send.at[s, 1], d_recv.at[s, 1], beside(4))
        push(mine, feat.at[s, 1], d_send.at[s, 2], d_recv.at[s, 2], beside(1))

    def forward(s):
        low, high = pl.ds(0, half), pl.ds(half, half)
        arrived(feat.at[s, 2], d_send.at[s, 0], d_recv.at[s, 0], beside(2))
        push(feat.at[s, 2, low], feat.at[s, 6, low], d_send.at[s, 3], d_recv.at[s, 3], beside(4))
        push(feat.at[s, 2], feat.at[s, 3], d_send.at[s, 5], d_recv.at[s, 5], beside(1))
        arrived(feat.at[s, 4], d_send.at[s, 1], d_recv.at[s, 1], beside(4))
        push(feat.at[s, 4, high], feat.at[s, 6, high], d_send.at[s, 4], d_recv.at[s, 4], beside(2))
        push(feat.at[s, 4], feat.at[s, 5], d_send.at[s, 6], d_recv.at[s, 6], beside(1))
        arrived(feat.at[s, 6, low], d_send.at[s, 3], d_recv.at[s, 3], beside(4))
        arrived(feat.at[s, 6, high], d_send.at[s, 4], d_recv.at[s, 4], beside(2))
        push(feat.at[s, 6], feat.at[s, 7], d_send.at[s, 7], d_recv.at[s, 7], beside(1))

    def complete(s):
        for rel, kind in ((1, 2), (3, 5), (5, 6), (7, 7)):
            arrived(feat.at[s, rel], d_send.at[s, kind], d_recv.at[s, kind], beside(1))

    def experts(s):
        wide = 512

        def choose(n, carry):
            at = pl.ds(pl.multiple_of(n * wide, wide), wide)
            found = [mm(pick_ref[s, rel], feat[s, rel, :, at]) for rel in range(8)]
            for j in range(2):
                routed[j, :, at] = jnp.concatenate(
                    [f[j * cap : (j + 1) * cap] for f in found], 0
                ).astype(BF)
            return carry

        lax.fori_loop(0, D // wide, choose, 0)
        if s == 0:
            for copy in loads:
                copy.wait()
        step = 256
        for j in range(2):

            def lift(n, carry):
                lo = pl.multiple_of(n * step, step)
                g = mm(routed[j], w_in[j, :, pl.ds(lo, step)])
                u = mm(routed[j], w_in[j, :, pl.ds(lo + FF, step)])
                units[j, :, pl.ds(lo, step)] = (g / (1.0 + jnp.exp(-g)) * u).astype(BF)
                return carry

            lax.fori_loop(0, FF // step, lift, 0)

        def lower(n, carry):
            at = pl.ds(pl.multiple_of(n * wide, wide), wide)
            y = [mm(units[j], w_out[j, :, at]) for j in range(2)]
            for rel in range(8):
                block = jnp.concatenate([v[rel * cap : (rel + 1) * cap] for v in y], 0).astype(BF)
                if rel == 0:
                    got[s, 0, :, at] = block
                else:
                    sent[s, rel, :, at] = block
            return carry

        lax.fori_loop(0, D // wide, lower, 0)
        for rel in (6, 7, 2, 4, 3, 5, 1):
            push(sent.at[s, rel], got.at[s, rel], r_send.at[s, rel], r_recv.at[s, rel], beside(rel))

    def combine(s):
        for rel in range(1, 8):
            arrived(got.at[s, rel], r_send.at[s, rel], r_recv.at[s, rel], beside(rel))
        wide = 512

        def mix(n, carry):
            at = pl.ds(pl.multiple_of(n * wide, wide), wide)
            part[s, :, at] = mm(
                weight_ref[s], got[s, :, :, at].reshape(8 * rows, wide)
            ).astype(BF)
            return carry

        lax.fori_loop(0, D // wide, mix, 0)
        if s:
            push(part.at[s], summed.at[s], p_send.at[s], p_recv.at[s], below(s))

    feat[0, 0] = x_ref[...]
    spread(0)
    for s in range(1, n_dp):
        push(feat.at[0, 0], feat.at[s, 0], z_send.at[s], z_recv.at[s], above(s))
    for s in range(n_dp):
        if s + 1 < n_dp:
            arrived(feat.at[s + 1, 0], z_send.at[s + 1], z_recv.at[s + 1], below(s + 1))
            spread(s + 1)
        forward(s)
        complete(s)
        experts(s)
        if s:
            combine(s - 1)
    combine(n_dp - 1)
    total = hidden_ref[...].astype(F32) + part[0].astype(F32)
    for s in range(1, n_dp):
        arrived(summed.at[s], p_send.at[s], p_recv.at[s], above(s))
        total = total + summed[s].astype(F32)
    o_ref[...] = total.astype(BF)
    for copy in started:
        copy.wait_send()


def moe(n_dp, expert_input, hidden_state, pick, weight, expert_in, expert_out):
    tokens = expert_input.shape[0]
    rows = pick.shape[2]
    vmem = pl.BlockSpec(memory_space=pltpu.VMEM)
    hbm = pl.BlockSpec(memory_space=pl.ANY)
    dma = pltpu.SemaphoreType.DMA
    return pl.pallas_call(
        functools.partial(moe_kernel, n_dp),
        out_shape=jax.ShapeDtypeStruct((tokens, D), BF),
        in_specs=[vmem, vmem, vmem, vmem, hbm, hbm],
        out_specs=vmem,
        scratch_shapes=[
            pltpu.VMEM((n_dp, 8, tokens, D), BF),
            pltpu.VMEM(expert_in.shape, BF),
            pltpu.VMEM(expert_out.shape, BF),
            pltpu.VMEM((2, 4 * rows, D), BF),
            pltpu.VMEM((2, 4 * rows, FF), BF),
            pltpu.VMEM((n_dp, 8, rows, D), BF),
            pltpu.VMEM((n_dp, 8, rows, D), BF),
            pltpu.VMEM((n_dp, tokens, D), BF),
            pltpu.VMEM((n_dp, tokens, D), BF),
            dma((2,)),
            dma((n_dp,)),
            dma((n_dp,)),
            dma((n_dp, 8)),
            dma((n_dp, 8)),
            dma((n_dp, 8)),
            dma((n_dp, 8)),
            dma((n_dp,)),
            dma((n_dp,)),
        ],
        compiler_params=pltpu.CompilerParams(
            collective_id=0, has_side_effects=True, vmem_limit_bytes=60 * 1024 * 1024
        ),
    )(expert_input, hidden_state, pick, weight, expert_in, expert_out)


def two_parts(a):
    high = lax.reduce_precision(a, 8, 7)
    return high.astype(BF), (a - high).astype(BF)


def slot_table(gate_rows, capacity):
    named = gate_rows > 0.0
    tokens = gate_rows.shape[-1]
    before = (
        jnp.arange(tokens, dtype=jnp.int32)[:, None] < jnp.arange(tokens, dtype=jnp.int32)[None, :]
    ).astype(BF)
    rank = jnp.einsum("...t,tu->...u", named.astype(BF), before, preferred_element_type=F32)
    slot = jnp.arange(capacity, dtype=jnp.int32).astype(F32)
    return named[..., None, :] & (rank[..., None, :] == slot[:, None])


def per_device(
    queries,
    key_in,
    value_in,
    gate_in,
    residual_in,
    log_decay,
    beta_logit,
    lengths,
    head_gain,
    out_proj,
    post_gain,
    expert_in,
    expert_out,
    routes,
    route_gates,
):
    tokens = queries.shape[1]
    n_ctx = lax.axis_size("ctx")
    n_dp = lax.axis_size("dp")
    local = expert_in.shape[0]
    devices = n_ctx * n_dp
    experts = local * devices
    capacity = tokens * TOPK * 6 // (5 * experts)
    group = HV // HK
    my_dp = lax.axis_index("dp")
    my_ctx = lax.axis_index("ctx")

    ids = jnp.arange(experts, dtype=jnp.int32)[:, None]
    gate_table = jnp.zeros((experts, tokens), F32)
    for k in range(TOPK):
        gate_table = gate_table + jnp.where(
            routes[0, :, k][None, :] == ids, route_gates[0, :, k][None, :], 0.0
        )
    gate_table = gate_table.astype(BF)
    column_gates = lax.all_gather(gate_table, "dp")
    gate_cols = gate_table.reshape(n_dp, n_ctx, local, tokens).transpose(1, 3, 0, 2)
    gate_cols = gate_cols.reshape(n_ctx, tokens, n_dp * local)

    beta = jax.nn.sigmoid(beta_logit[0])
    dh, dl = two_parts(log_decay[0])
    bh, bl = two_parts(beta)
    scal = jnp.stack([dh, dl, bh, bl]).reshape(4, n_ctx, group, tokens)
    scal = scal.transpose(1, 3, 0, 2).reshape(n_ctx, tokens, 4 * group)
    scal = jnp.concatenate([scal, gate_cols], -1)
    scal = jnp.pad(scal, ((0, 0), (0, 0), (0, SCAL - scal.shape[-1])))

    def by_head(a):
        return a[0].reshape(tokens, n_ctx, -1).transpose(1, 0, 2)

    sent = jnp.concatenate([by_head(queries), by_head(key_in), by_head(value_in), scal], -1)
    heads = lax.all_to_all(sent, "ctx", split_axis=0, concat_axis=0, tiled=True)
    gates_at = 2 * DK + group * DV + 4 * group
    plane_gates = lax.all_gather(heads[:, :, gates_at : gates_at + n_dp * local], "dp")
    mixed = mixer(lengths, heads.reshape(n_ctx * tokens, -1), head_gain)
    mine = lax.all_to_all(
        mixed.reshape(n_ctx, tokens, group * DV), "ctx", split_axis=0, concat_axis=0, tiled=True
    )
    unit = mine.transpose(1, 0, 2).reshape(tokens, HV * DV)
    normed = (unit.astype(F32) * jax.nn.silu(gate_in[0].astype(F32))).astype(BF)
    projected = jnp.dot(normed, out_proj, preferred_element_type=F32)
    hidden_state = (residual_in[0].astype(F32) + projected).astype(BF)
    expert_input = post_norm(hidden_state, post_gain)

    packs = (my_dp - jnp.arange(n_dp)) % n_dp
    places = my_ctx ^ jnp.arange(n_ctx)
    my_gates = plane_gates.reshape(n_dp, n_ctx, tokens, n_dp, local)
    my_gates = lax.dynamic_index_in_dim(my_gates, my_dp, 3, False).transpose(0, 1, 3, 2)
    my_gates = my_gates[packs][:, places]
    pick = slot_table(my_gates, capacity).astype(BF)
    pick = pick.reshape(n_dp, n_ctx, local * capacity, tokens)
    plane = column_gates.reshape(n_dp, n_dp, n_ctx, local, tokens)
    plane = lax.dynamic_index_in_dim(plane, my_dp, 1, False)[packs][:, places]
    weight = jnp.where(slot_table(plane, capacity), plane[..., None, :], 0)
    weight = weight.reshape(n_dp, n_ctx * local * capacity, tokens).transpose(0, 2, 1)
    return moe(n_dp, expert_input, hidden_state, pick, weight, expert_in, expert_out)[None]


def solution(mesh):
    in_specs = (
        P("dp", "ctx", None),
        P("dp", "ctx", None),
        P("dp", "ctx", None),
        P("dp", "ctx", None),
        P("dp", "ctx", None),
        P("dp", None, "ctx"),
        P("dp", None, "ctx"),
        P("dp", None),
        P(),
        P(),
        P(),
        P(("dp", "ctx"), None, None),
        P(("dp", "ctx"), None, None),
        P("dp", "ctx", None),
        P("dp", "ctx", None),
    )
    out_specs = P("dp", "ctx", None)
    by_heads = mesh.shape["ctx"] == HK
    return jax.shard_map(
        per_device if by_heads else per_device_long, mesh=mesh, in_specs=in_specs, out_specs=out_specs, check_vma=False
    )
```

```python
import functools

import jax
import jax.numpy as jnp
from jax import lax
from jax.experimental import pallas as pl
from jax.experimental.pallas import tpu as pltpu
from jax.sharding import PartitionSpec as P

D = 2048
DK = 128
DV = 128
FF = 512
TOPK = 10
HK = 8
HV = 16
BLOCK = 64


EPSILON = 1e-06
HIGHEST = lax.Precision.HIGHEST
ROWWISE = lax.Precision.HIGH


def entering(part, axis, combine, identity):
    place = lax.axis_index(axis)
    gathered = jax.tree.map(lambda a: lax.all_gather(a, axis), part)
    state = jax.tree.map(lambda a, e: jnp.zeros_like(a) + jnp.asarray(e, a.dtype), part, identity)

    def one(lap, state):
        return combine(
            state, jax.tree.map(lambda a: lax.dynamic_index_in_dim(a, lap, 0, False), gathered)
        )

    return lax.fori_loop(0, place, one, state)


def unit_heads(matrix, head_count, factor):
    shaped = matrix.astype(jnp.float32).reshape(matrix.shape[0], head_count, -1)
    return shaped * lax.rsqrt(jnp.sum(shaped * shaped, -1, keepdims=True) + EPSILON) * factor


def segment_of(lengths, positions):
    starts = jnp.cumsum(lengths) - lengths
    return jnp.sum((starts[:, None] <= positions[None, :]).astype(jnp.int32), 0) - 1


def block_terms(queries, key_rows, value_rows, beta_gate, decay_log, segment, seg_before):
    length = key_rows.shape[1]
    cumulative = jnp.cumsum(decay_log, axis=-1)
    rows_at = jnp.arange(length)[:, None]
    cols_at = jnp.arange(length)[None, :]
    same_doc = (segment[:, None] == segment[None, :]) & (rows_at >= cols_at)
    log_gap = jnp.minimum(cumulative[:, :, None] - cumulative[:, None, :], 0.0)
    decay_pair = jnp.where(same_doc[None], jnp.exp(log_gap), 0.0)
    from_start = jnp.where((segment == seg_before)[None, :], jnp.exp(cumulative), 0.0)
    to_end = decay_pair[:, -1, :]
    key_inner = jnp.einsum("hcd,hsd->hcs", key_rows, key_rows, precision=ROWWISE)
    lower_part = jnp.where(
        (rows_at > cols_at)[None], beta_gate[:, :, None] * decay_pair * key_inner, 0.0
    )
    system = jnp.eye(length, dtype=jnp.float32)[None] + lower_part
    right_side = jnp.concatenate(
        [beta_gate[:, :, None] * value_rows, (beta_gate * from_start)[:, :, None] * key_rows],
        axis=-1,
    )
    solved = jax.scipy.linalg.solve_triangular(system, right_side, lower=True, unit_diagonal=True)
    value_width = value_rows.shape[-1]
    pseudo = solved[..., :value_width]
    weights = solved[..., value_width:]
    scores = jnp.einsum("hcd,hsd->hcs", queries, key_rows, precision=ROWWISE) * decay_pair
    weighted = key_rows * to_end[:, :, None]
    key_width = key_rows.shape[-1]
    transition = from_start[:, -1][:, None, None] * jnp.eye(key_width, dtype=jnp.float32)[
        None
    ] - jnp.einsum("hcd,hce->hde", weighted, weights, precision=HIGHEST)
    offset = jnp.einsum("hcd,hce->hde", weighted, pseudo, precision=HIGHEST)
    return (pseudo, weights, scores, from_start, transition, offset)


def block_output(queries, pseudo, weights, scores, from_start, carried):
    errors = pseudo - jnp.einsum("hcd,hde->hce", weights, carried, precision=ROWWISE)
    return jnp.einsum(
        "hcd,hde->hce", queries * from_start[:, :, None], carried, precision=ROWWISE
    ) + jnp.einsum("hcs,hse->hce", scores, errors, precision=ROWWISE)


def apply_map(transition, carried):
    return jnp.einsum("hde,hef->hdf", transition, carried, precision=HIGHEST)


def head_blocks(matrix, block_len):
    length, head_count, inner_width = matrix.shape
    return matrix.reshape(length // block_len, block_len, head_count, inner_width).transpose(
        0, 2, 1, 3
    )


def prepare(queries, key_in, value_in, log_decay, beta_logit, segment, seg_before):
    length = queries.shape[0]
    group_size = HV // HK
    query_heads = jnp.repeat(unit_heads(queries, HK, DK ** (-0.5)), group_size, axis=1)
    key_heads = jnp.repeat(unit_heads(key_in, HK, 1.0), group_size, axis=1)
    value_heads = value_in.astype(jnp.float32).reshape(length, HV, DV)
    nblock = length // BLOCK
    beta_gate = jax.nn.sigmoid(beta_logit).reshape(HV, nblock, BLOCK).transpose(1, 0, 2)
    decay_log = log_decay.reshape(HV, nblock, BLOCK).transpose(1, 0, 2)
    seg_blocks = segment.reshape(nblock, BLOCK)
    seg_starts = jnp.concatenate([jnp.reshape(seg_before, (1,)), seg_blocks[:-1, -1]])
    query_blocks = head_blocks(query_heads, BLOCK)
    terms = jax.vmap(block_terms)(
        query_blocks,
        head_blocks(key_heads, BLOCK),
        head_blocks(value_heads, BLOCK),
        beta_gate,
        decay_log,
        seg_blocks,
        seg_starts,
    )
    return (query_blocks, terms)


def finish(query_blocks, terms, start_state, gate_in, residual_in, head_gain, out_proj):
    pseudo, weights, scores, from_start, transition, offset = terms

    def advance(carried, member):
        return (apply_map(member[0], carried) + member[1], carried)

    final_state, block_starts = lax.scan(advance, start_state, (transition, offset))
    outputs = jax.vmap(block_output)(
        query_blocks, pseudo, weights, scores, from_start, block_starts
    )
    length = gate_in.shape[0]
    outputs = outputs.transpose(0, 2, 1, 3).reshape(length, HV, DV)
    mean_square = jnp.mean(outputs * outputs, -1, keepdims=True)
    gate_heads = gate_in.astype(jnp.float32).reshape(length, HV, DV)
    normed = (
        (outputs * lax.rsqrt(mean_square + EPSILON) * head_gain * jax.nn.silu(gate_heads))
        .reshape(length, HV * DV)
        .astype(jnp.bfloat16)
    )
    mixed = jnp.dot(normed, out_proj, preferred_element_type=jnp.float32)
    return (residual_in.astype(jnp.float32) + mixed).astype(jnp.bfloat16)


def post_norm(hidden_state, post_gain):
    widened = hidden_state.astype(jnp.float32)
    return (
        widened * lax.rsqrt(jnp.mean(widened * widened, -1, keepdims=True) + EPSILON) * post_gain
    ).astype(jnp.bfloat16)


def rank_of(flat_ids, experts):
    onehot = (flat_ids[:, None] == jnp.arange(experts, dtype=jnp.int32)[None, :]).astype(jnp.int32)
    return jnp.sum((jnp.cumsum(onehot, 0) - onehot) * onehot, 1)


def expert_apply(routed, expert_in, expert_out):
    gate_up = jnp.einsum("sjcd,jdf->sjcf", routed, expert_in, preferred_element_type=jnp.float32)
    hidden_units = (jax.nn.silu(gate_up[..., :FF]) * gate_up[..., FF:]).astype(jnp.bfloat16)
    return jnp.einsum(
        "sjcf,jfd->sjcd", hidden_units, expert_out, preferred_element_type=jnp.float32
    ).astype(jnp.bfloat16)


def per_device_long(
    queries,
    key_in,
    value_in,
    gate_in,
    residual_in,
    log_decay,
    beta_logit,
    lengths,
    head_gain,
    out_proj,
    post_gain,
    expert_in,
    expert_out,
    routes,
    route_gates,
):
    tokens_dev = queries.shape[1]
    ctx_index = lax.axis_index("ctx")
    positions = ctx_index * tokens_dev + jnp.arange(tokens_dev, dtype=jnp.int32)
    segment = segment_of(lengths[0], positions)
    previous = segment_of(lengths[0], jnp.reshape(positions[0] - 1, (1,)))[0]
    seg_before = jnp.where(ctx_index > 0, previous, -1)
    query_blocks, terms = prepare(
        queries[0], key_in[0], value_in[0], log_decay[0], beta_logit[0], segment, seg_before
    )
    eye_maps = jnp.broadcast_to(jnp.eye(DK, dtype=jnp.float32), (HV, DK, DK))
    zero_offset = jnp.zeros((HV, DK, DV), jnp.float32)

    def compose(carry_pair, member):
        return (
            (apply_map(member[0], carry_pair[0]), apply_map(member[0], carry_pair[1]) + member[1]),
            None,
        )

    device_pair, unused = lax.scan(compose, (eye_maps, zero_offset), (terms[4], terms[5]))

    def combine(earlier, later):
        return (apply_map(later[0], earlier[0]), apply_map(later[0], earlier[1]) + later[1])

    prefix_map, prefix_offset = entering(
        (device_pair[0], device_pair[1]), "ctx", combine, (eye_maps, zero_offset)
    )
    hidden_state = finish(
        query_blocks, terms, prefix_offset, gate_in[0], residual_in[0], head_gain, out_proj
    )
    expert_input = post_norm(hidden_state, post_gain)
    local_experts = expert_in.shape[0]
    device_count = lax.axis_size("dp") * lax.axis_size("ctx")
    experts_all = local_experts * device_count
    capacity = tokens_dev * TOPK * 6 // (5 * experts_all)
    flat_ids = routes[0].reshape(-1)
    slot_rank = rank_of(flat_ids, experts_all)
    outbound = (
        jnp.zeros((experts_all, capacity, D), jnp.bfloat16)
        .at[flat_ids, slot_rank]
        .set(jnp.repeat(expert_input, TOPK, axis=0))
    )
    outbound = outbound.reshape(device_count, local_experts, capacity, D)
    computed = expert_apply(
        lax.all_to_all(outbound, ("dp", "ctx"), split_axis=0, concat_axis=0, tiled=True),
        expert_in,
        expert_out,
    )
    returned = lax.all_to_all(computed, ("dp", "ctx"), split_axis=0, concat_axis=0, tiled=True)
    back_rows = returned.reshape(experts_all, capacity, D)[flat_ids, slot_rank]
    expert_mix = jnp.sum(
        back_rows.astype(jnp.float32).reshape(tokens_dev, TOPK, D) * route_gates[0][:, :, None], 1
    )
    summed = hidden_state.astype(jnp.float32) + expert_mix
    return summed.astype(jnp.bfloat16)[None]


TILE = 128
SCAL = 128
BF = jnp.bfloat16
F32 = jnp.float32


def mm(a, b):
    return jnp.dot(a, b, preferred_element_type=F32)


def mm_nt(a, b):
    return lax.dot_general(a, b, (((1,), (1,)), ((), ())), preferred_element_type=F32)


def halves(a):
    high = a.astype(BF)
    return high, (a - high.astype(F32)).astype(BF)


def dot3(a, b):
    ah, al = a
    bh, bl = b
    return mm(ah, bh) + (mm(ah, bl) + mm(al, bh))


def mixer_kernel(lengths_ref, x_ref, gain_ref, out_ref, pseudo, weights, scores, keyed, ends):
    total = x_ref.shape[0]
    tiles = total // TILE
    group = HV // HK
    rows = lax.broadcasted_iota(jnp.int32, (TILE, TILE), 0)
    cols = lax.broadcasted_iota(jnp.int32, (TILE, TILE), 1)
    eye = (rows == cols).astype(F32)
    tri = (rows >= cols).astype(BF)
    starts = []
    at = jnp.int32(0)
    for j in range(lengths_ref.shape[1]):
        starts.append(at)
        at = at + lengths_ref[0, j]

    def segment(pos):
        seg = jnp.zeros(pos.shape, jnp.int32)
        for start in starts:
            seg = seg + (start <= pos).astype(jnp.int32)
        return seg

    def terms_of(tile):
        base = pl.multiple_of(tile * TILE, TILE)
        q = x_ref[pl.ds(base, TILE), 0:DK]
        k = x_ref[pl.ds(base, TILE), DK : 2 * DK]
        sc = x_ref[pl.ds(base, TILE), 2 * DK + group * DV : 2 * DK + group * DV + SCAL]
        cum = mm(tri, sc)
        qf = q.astype(F32)
        kf = k.astype(F32)
        rq = lax.rsqrt(jnp.sum(qf * qf, -1, keepdims=True) + EPSILON) * DK ** (-0.5)
        rk = lax.rsqrt(jnp.sum(kf * kf, -1, keepdims=True) + EPSILON)
        scf = sc.astype(F32)
        seg_c = segment(base + rows)
        seg_r = segment(base + cols)
        seg_b = segment(jnp.full((TILE, 1), base - 1, jnp.int32))
        causal = (seg_c == seg_r) & (rows >= cols)
        open_c = (seg_c[:, :1] == seg_b) & (base > 0)
        g_c, beta_c, from_c = [], [], []
        for h in range(group):
            g = cum[:, h : h + 1] + cum[:, group + h : group + h + 1]
            b = (
                scf[:, 2 * group + h : 2 * group + h + 1]
                + scf[:, 3 * group + h : 3 * group + h + 1]
            )
            g_c.append(g)
            beta_c.append(b)
            from_c.append(jnp.where(open_c, jnp.exp(g), 0.0))
        packed = jnp.zeros((TILE, TILE), F32)
        for n, col in enumerate(g_c + beta_c + from_c + [rk]):
            packed = jnp.where(cols == n, col, packed)
        flat = packed.T
        rk_r = flat[3 * group : 3 * group + 1, :]
        kk = mm_nt(k, k) * rk * rk_r
        qk = mm_nt(q, k) * rq * rk_r
        per_head = []
        for h in range(group):
            g_r = flat[h : h + 1, :]
            beta_r = flat[group + h : group + h + 1, :]
            from_r = flat[2 * group + h : 2 * group + h + 1, :]
            pair = jnp.where(causal, jnp.exp(jnp.minimum(g_c[h] - g_r, 0.0)), 0.0)
            lower = jnp.where(rows > cols, beta_c[h] * pair * kk, 0.0)
            last = jnp.where(
                (seg_c[TILE - 1 :, :1] == seg_c[:, :1]),
                jnp.exp(jnp.minimum(g_c[h][TILE - 1 :, :] - g_c[h], 0.0)),
                0.0,
            )
            per_head.append(
                dict(
                    tile=tile,
                    h=h,
                    base=base,
                    lower=lower,
                    score=qk * pair,
                    beta_r=beta_r,
                    scale_r=beta_r * from_r * rk_r,
                    k=k,
                    to_end=last * rk,
                    read=from_c[h] * rq,
                    from_end=from_c[h][TILE - 1 :, :],
                )
            )
        return per_head

    def build(step, carry):
        work = []
        for u in range(2):
            work += terms_of(step * 2 + u)
        near = ((rows ^ cols) == 1) & (rows > cols)
        inverse = [eye - jnp.where(near, w["lower"], 0.0) for w in work]
        level = 1
        while (1 << level) < TILE:
            mask = (((rows >> level) ^ (cols >> level)) == 1) & (rows > cols)
            parts = [halves(x) for x in inverse]
            links = [halves(jnp.where(mask, w["lower"], 0.0)) for w in work]
            first = [halves(dot3(x, c)) for x, c in zip(parts, links)]
            inverse = [x - dot3(f, p) for x, f, p in zip(inverse, first, parts)]
            level += 1
        for w, x in zip(work, inverse):
            slot = w["tile"] * group + w["h"]
            v = x_ref[
                pl.ds(w["base"], TILE), 2 * DK + w["h"] * DV : 2 * DK + (w["h"] + 1) * DV
            ]
            xh, xl = halves(x * w["beta_r"])
            pseudo[slot] = mm(xh, v) + mm(xl, v)
            wh, wl = halves(x * w["scale_r"])
            weights[slot] = mm(wh, w["k"]) + mm(wl, w["k"])
            scores[slot] = w["score"]
            keyed[slot] = jnp.where(cols == 0, w["to_end"], jnp.where(cols == 1, w["read"], 0.0))
            ends[slot] = jnp.broadcast_to(w["from_end"], (8, TILE))
        return carry

    lax.fori_loop(0, tiles // 2, build, 0)

    def advance(tile, states):
        base = pl.multiple_of(tile * TILE, TILE)
        q = x_ref[pl.ds(base, TILE), 0:DK]
        k = x_ref[pl.ds(base, TILE), DK : 2 * DK]
        following = []
        for h in range(group):
            slot = tile * group + h
            state = states[h]
            sh, sl = halves(state)
            error = pseudo[slot] - dot3(halves(weights[slot]), (sh, sl))
            scalars = keyed[slot]
            eh, el = halves(error * scalars[:, 0:1])
            grown = lax.dot_general(
                k, eh, (((0,), (0,)), ((), ())), preferred_element_type=F32
            ) + lax.dot_general(k, el, (((0,), (0,)), ((), ())), preferred_element_type=F32)
            following.append(ends[slot][0:1, :] * state + grown)
            raw = (mm(q, sh) + mm(q, sl)) * scalars[:, 1:2] + dot3(
                halves(scores[slot]), halves(error)
            )
            mean = jnp.mean(raw * raw, -1, keepdims=True)
            out_ref[pl.ds(base, TILE), h * DV : (h + 1) * DV] = (
                raw * lax.rsqrt(mean + EPSILON) * gain_ref[...]
            ).astype(BF)
        return tuple(following)

    lax.fori_loop(
        0, tiles, advance, tuple(jnp.zeros((DK, DV), F32) for h in range(group))
    )


def mixer(lengths, rows, head_gain):
    total = rows.shape[0]
    group = HV // HK
    slots = total // TILE * group
    vmem = pl.BlockSpec(memory_space=pltpu.VMEM)
    return pl.pallas_call(
        mixer_kernel,
        out_shape=jax.ShapeDtypeStruct((total, group * DV), BF),
        in_specs=[pl.BlockSpec(memory_space=pltpu.SMEM), vmem, vmem],
        out_specs=vmem,
        scratch_shapes=[
            pltpu.VMEM((slots, TILE, DV), F32),
            pltpu.VMEM((slots, TILE, DK), F32),
            pltpu.VMEM((slots, TILE, TILE), F32),
            pltpu.VMEM((slots, TILE, TILE), F32),
            pltpu.VMEM((slots, 8, TILE), F32),
        ],
        compiler_params=pltpu.CompilerParams(vmem_limit_bytes=40 * 1024 * 1024),
    )(lengths, rows, head_gain.reshape(1, DV))


def moe_kernel(
    n_dp, x_ref, hidden_ref, pick_ref, weight_ref, in_hbm, out_hbm, o_ref,
    feat, w_in, w_out, routed, units, sent, got, part, summed,
    load_sem, z_send, z_recv, d_send, d_recv, r_send, r_recv, p_send, p_recv,
):
    z = lax.axis_index("dp")
    me = lax.axis_index("ctx")
    tokens = x_ref.shape[0]
    half = tokens // 2
    rows = sent.shape[2]
    cap = rows // 2
    core, along_x, along_y = me % 2, (me // 2) % 2, me // 4

    def beside(rel):
        c = 1 - core if rel % 2 else core
        x = 1 - along_x if (rel // 2) % 2 else along_x
        y = 1 - along_y if rel // 4 else along_y
        return (z, (y * 2 + x) * 2 + c)

    far = z // 2
    inner = z + far * (3 - 2 * z)
    order = [d + far * (3 - 2 * d) for d in (inner, 1 - inner, 2, 3)]
    inward = (z + 1 - 2 * far, me)
    outward = (lax.rem(z + n_dp - 1 + 2 * far, n_dp), me)

    loads = [
        pltpu.make_async_copy(in_hbm, w_in, load_sem.at[0]),
        pltpu.make_async_copy(out_hbm, w_out, load_sem.at[1]),
    ]
    for copy in loads:
        copy.start()
    barrier = pltpu.get_barrier_semaphore()
    peers = [(lax.rem(z + s, n_dp), me) for s in range(1, n_dp)] + [beside(rel) for rel in range(1, 8)]
    for peer in peers:
        pl.semaphore_signal(barrier, inc=1, device_id=peer, device_id_type=pl.DeviceIdType.MESH)
    pl.semaphore_wait(barrier, len(peers))

    started = []

    def push(src, dst, send, recv, peer):
        copy = pltpu.make_async_remote_copy(
            src_ref=src, dst_ref=dst, send_sem=send, recv_sem=recv,
            device_id=peer, device_id_type=pl.DeviceIdType.MESH,
        )
        copy.start()
        started.append(copy)

    def arrived(dst, send, recv, peer):
        pltpu.make_async_remote_copy(
            src_ref=dst, dst_ref=dst, send_sem=send, recv_sem=recv,
            device_id=peer, device_id_type=pl.DeviceIdType.MESH,
        ).wait_recv()

    def spread(s):
        mine = feat.at[s, 0]
        push(mine, feat.at[s, 2], d_send.at[s, 0], d_recv.at[s, 0], beside(2))
        push(mine, feat.at[s, 4], d_send.at[s, 1], d_recv.at[s, 1], beside(4))
        push(mine, feat.at[s, 1], d_send.at[s, 2], d_recv.at[s, 2], beside(1))

    def forward(s):
        low, high = pl.ds(0, half), pl.ds(half, half)
        arrived(feat.at[s, 2], d_send.at[s, 0], d_recv.at[s, 0], beside(2))
        push(feat.at[s, 2, low], feat.at[s, 6, low], d_send.at[s, 3], d_recv.at[s, 3], beside(4))
        push(feat.at[s, 2], feat.at[s, 3], d_send.at[s, 5], d_recv.at[s, 5], beside(1))
        arrived(feat.at[s, 4], d_send.at[s, 1], d_recv.at[s, 1], beside(4))
        push(feat.at[s, 4, high], feat.at[s, 6, high], d_send.at[s, 4], d_recv.at[s, 4], beside(2))
        push(feat.at[s, 4], feat.at[s, 5], d_send.at[s, 6], d_recv.at[s, 6], beside(1))
        arrived(feat.at[s, 6, low], d_send.at[s, 3], d_recv.at[s, 3], beside(4))
        arrived(feat.at[s, 6, high], d_send.at[s, 4], d_recv.at[s, 4], beside(2))
        push(feat.at[s, 6], feat.at[s, 7], d_send.at[s, 7], d_recv.at[s, 7], beside(1))

    def complete(s):
        for rel, kind in ((1, 2), (3, 5), (5, 6), (7, 7)):
            arrived(feat.at[s, rel], d_send.at[s, kind], d_recv.at[s, kind], beside(1))

    def experts(s, load):
        wide = 512

        def choose(n, carry):
            at = pl.ds(pl.multiple_of(n * wide, wide), wide)
            found = [mm(pick_ref[s, rel], feat[s, rel, :, at]) for rel in range(8)]
            for j in range(2):
                routed[j, :, at] = jnp.concatenate(
                    [f[j * cap : (j + 1) * cap] for f in found], 0
                ).astype(BF)
            return carry

        lax.fori_loop(0, D // wide, choose, 0)
        if load:
            for copy in loads:
                copy.wait()
        step = 256
        for j in range(2):

            def lift(n, carry):
                lo = pl.multiple_of(n * step, step)
                g = mm(routed[j], w_in[j, :, pl.ds(lo, step)])
                u = mm(routed[j], w_in[j, :, pl.ds(lo + FF, step)])
                units[j, :, pl.ds(lo, step)] = (g / (1.0 + jnp.exp(-g)) * u).astype(BF)
                return carry

            lax.fori_loop(0, FF // step, lift, 0)

        def lower(n, carry):
            at = pl.ds(pl.multiple_of(n * wide, wide), wide)
            y = [mm(units[j], w_out[j, :, at]) for j in range(2)]
            for rel in range(8):
                block = jnp.concatenate([v[rel * cap : (rel + 1) * cap] for v in y], 0).astype(BF)
                if rel == 0:
                    got[s, 0, :, at] = block
                else:
                    sent[s, rel, :, at] = block
            return carry

        lax.fori_loop(0, D // wide, lower, 0)
        for rel in (6, 7, 2, 4, 3, 5, 1):
            push(sent.at[s, rel], got.at[s, rel], r_send.at[s, rel], r_recv.at[s, rel], beside(rel))

    def combine(s, remote):
        for rel in range(1, 8):
            arrived(got.at[s, rel], r_send.at[s, rel], r_recv.at[s, rel], beside(rel))
        wide = 512

        def mix(n, carry):
            at = pl.ds(pl.multiple_of(n * wide, wide), wide)
            part[s, :, at] = mm(
                weight_ref[s], got[s, :, :, at].reshape(8 * rows, wide)
            ).astype(BF)
            return carry

        lax.fori_loop(0, D // wide, mix, 0)
        if remote:
            push(part.at[s], summed.at[z], p_send.at[s], p_recv.at[z], (s, me))

    def along(place, slot, peer):
        d = order[place]
        return pltpu.make_async_remote_copy(
            src_ref=feat.at[d, 0], dst_ref=feat.at[d, 0], send_sem=z_send.at[slot],
            recv_sem=z_recv.at[d], device_id=peer, device_id_type=pl.DeviceIdType.MESH,
        )

    def take(place):
        d = order[place]
        along(place, 0, inward).wait_recv()

        @pl.when(inner == 1)
        def pass_on():
            along(place, place + 1, inward if place == 1 else outward).start()

        spread(d)

    own, first, second, third = order
    feat[own, 0] = x_ref[...]
    along(0, 0, inward).start()

    @pl.when(inner == 1)
    def both_ways():
        along(0, 1, outward).start()

    spread(own)
    take(1)
    forward(own)
    take(2)
    forward(first)
    take(3)
    complete(first)
    experts(first, True)
    forward(second)
    complete(second)
    experts(second, False)
    forward(third)
    complete(third)
    experts(third, False)
    combine(first, True)
    complete(own)
    experts(own, False)
    combine(second, True)
    combine(third, True)
    combine(own, False)
    total = hidden_ref[...].astype(F32) + part[own].astype(F32)
    for d in (first, second, third):
        arrived(summed.at[d], p_send.at[d], p_recv.at[d], (d, me))
        total = total + summed[d].astype(F32)
    o_ref[...] = total.astype(BF)
    along(0, 0, inward).wait_send()

    @pl.when(inner == 1)
    def passed():
        along(0, 1, outward).wait_send()
        for place in range(1, n_dp):
            along(place, place + 1, inward if place == 1 else outward).wait_send()

    for copy in started:
        copy.wait_send()


def moe(n_dp, expert_input, hidden_state, pick, weight, expert_in, expert_out):
    tokens = expert_input.shape[0]
    rows = pick.shape[2]
    vmem = pl.BlockSpec(memory_space=pltpu.VMEM)
    hbm = pl.BlockSpec(memory_space=pl.ANY)
    dma = pltpu.SemaphoreType.DMA
    return pl.pallas_call(
        functools.partial(moe_kernel, n_dp),
        out_shape=jax.ShapeDtypeStruct((tokens, D), BF),
        in_specs=[vmem, vmem, vmem, vmem, hbm, hbm],
        out_specs=vmem,
        scratch_shapes=[
            pltpu.VMEM((n_dp, 8, tokens, D), BF),
            pltpu.VMEM(expert_in.shape, BF),
            pltpu.VMEM(expert_out.shape, BF),
            pltpu.VMEM((2, 4 * rows, D), BF),
            pltpu.VMEM((2, 4 * rows, FF), BF),
            pltpu.VMEM((n_dp, 8, rows, D), BF),
            pltpu.VMEM((n_dp, 8, rows, D), BF),
            pltpu.VMEM((n_dp, tokens, D), BF),
            pltpu.VMEM((n_dp, tokens, D), BF),
            dma((2,)),
            dma((n_dp + 1,)),
            dma((n_dp,)),
            dma((n_dp, 8)),
            dma((n_dp, 8)),
            dma((n_dp, 8)),
            dma((n_dp, 8)),
            dma((n_dp,)),
            dma((n_dp,)),
        ],
        compiler_params=pltpu.CompilerParams(
            collective_id=0, has_side_effects=True, vmem_limit_bytes=60 * 1024 * 1024
        ),
    )(expert_input, hidden_state, pick, weight, expert_in, expert_out)


def two_parts(a):
    high = lax.reduce_precision(a, 8, 7)
    return high.astype(BF), (a - high).astype(BF)


def slot_table(gate_rows, capacity):
    named = gate_rows > 0.0
    tokens = gate_rows.shape[-1]
    before = (
        jnp.arange(tokens, dtype=jnp.int32)[:, None] < jnp.arange(tokens, dtype=jnp.int32)[None, :]
    ).astype(BF)
    rank = jnp.einsum("...t,tu->...u", named.astype(BF), before, preferred_element_type=F32)
    slot = jnp.arange(capacity, dtype=jnp.int32).astype(F32)
    return named[..., None, :] & (rank[..., None, :] == slot[:, None])


def per_device(
    queries,
    key_in,
    value_in,
    gate_in,
    residual_in,
    log_decay,
    beta_logit,
    lengths,
    head_gain,
    out_proj,
    post_gain,
    expert_in,
    expert_out,
    routes,
    route_gates,
):
    tokens = queries.shape[1]
    n_ctx = lax.axis_size("ctx")
    n_dp = lax.axis_size("dp")
    local = expert_in.shape[0]
    devices = n_ctx * n_dp
    experts = local * devices
    capacity = tokens * TOPK * 6 // (5 * experts)
    group = HV // HK
    my_dp = lax.axis_index("dp")
    my_ctx = lax.axis_index("ctx")

    ids = jnp.arange(experts, dtype=jnp.int32)[:, None]
    gate_table = jnp.zeros((experts, tokens), F32)
    for k in range(TOPK):
        gate_table = gate_table + jnp.where(
            routes[0, :, k][None, :] == ids, route_gates[0, :, k][None, :], 0.0
        )
    gate_table = gate_table.astype(BF)
    column_gates = lax.all_gather(gate_table, "dp")
    gate_cols = gate_table.reshape(n_dp, n_ctx, local, tokens).transpose(1, 3, 0, 2)
    gate_cols = gate_cols.reshape(n_ctx, tokens, n_dp * local)

    beta = jax.nn.sigmoid(beta_logit[0])
    dh, dl = two_parts(log_decay[0])
    bh, bl = two_parts(beta)
    scal = jnp.stack([dh, dl, bh, bl]).reshape(4, n_ctx, group, tokens)
    scal = scal.transpose(1, 3, 0, 2).reshape(n_ctx, tokens, 4 * group)
    scal = jnp.concatenate([scal, gate_cols], -1)
    scal = jnp.pad(scal, ((0, 0), (0, 0), (0, SCAL - scal.shape[-1])))

    def by_head(a):
        return a[0].reshape(tokens, n_ctx, -1).transpose(1, 0, 2)

    sent = jnp.concatenate([by_head(queries), by_head(key_in), by_head(value_in), scal], -1)
    heads = lax.all_to_all(sent, "ctx", split_axis=0, concat_axis=0, tiled=True)
    gates_at = 2 * DK + group * DV + 4 * group
    plane_gates = lax.all_gather(heads[:, :, gates_at : gates_at + n_dp * local], "dp")
    mixed = mixer(lengths, heads.reshape(n_ctx * tokens, -1), head_gain)
    mine = lax.all_to_all(
        mixed.reshape(n_ctx, tokens, group * DV), "ctx", split_axis=0, concat_axis=0, tiled=True
    )
    unit = mine.transpose(1, 0, 2).reshape(tokens, HV * DV)
    normed = (unit.astype(F32) * jax.nn.silu(gate_in[0].astype(F32))).astype(BF)
    projected = jnp.dot(normed, out_proj, preferred_element_type=F32)
    hidden_state = (residual_in[0].astype(F32) + projected).astype(BF)
    expert_input = post_norm(hidden_state, post_gain)

    places = my_ctx ^ jnp.arange(n_ctx)
    my_gates = plane_gates.reshape(n_dp, n_ctx, tokens, n_dp, local)
    my_gates = lax.dynamic_index_in_dim(my_gates, my_dp, 3, False).transpose(0, 1, 3, 2)
    my_gates = my_gates[:, places]
    pick = slot_table(my_gates, capacity).astype(BF)
    pick = pick.reshape(n_dp, n_ctx, local * capacity, tokens)
    plane = column_gates.reshape(n_dp, n_dp, n_ctx, local, tokens)
    plane = lax.dynamic_index_in_dim(plane, my_dp, 1, False)[:, places]
    weight = jnp.where(slot_table(plane, capacity), plane[..., None, :], 0)
    weight = weight.reshape(n_dp, n_ctx * local * capacity, tokens).transpose(0, 2, 1)
    return moe(n_dp, expert_input, hidden_state, pick, weight, expert_in, expert_out)[None]


def solution(mesh):
    in_specs = (
        P("dp", "ctx", None),
        P("dp", "ctx", None),
        P("dp", "ctx", None),
        P("dp", "ctx", None),
        P("dp", "ctx", None),
        P("dp", None, "ctx"),
        P("dp", None, "ctx"),
        P("dp", None),
        P(),
        P(),
        P(),
        P(("dp", "ctx"), None, None),
        P(("dp", "ctx"), None, None),
        P("dp", "ctx", None),
        P("dp", "ctx", None),
    )
    out_specs = P("dp", "ctx", None)
    by_heads = mesh.shape["ctx"] == HK and mesh.shape["dp"] == 4
    return jax.shard_map(
        per_device if by_heads else per_device_long, mesh=mesh, in_specs=in_specs, out_specs=out_specs, check_vma=False
    )
```

```python
import functools

import jax
import jax.numpy as jnp
from jax import lax
from jax.experimental import pallas as pl
from jax.experimental.pallas import tpu as pltpu
from jax.sharding import PartitionSpec as P

D = 2048
DK = 128
DV = 128
FF = 512
TOPK = 10
HK = 8
HV = 16
BLOCK = 64


EPSILON = 1e-06
HIGHEST = lax.Precision.HIGHEST
ROWWISE = lax.Precision.HIGH


def entering(part, axis, combine, identity):
    place = lax.axis_index(axis)
    gathered = jax.tree.map(lambda a: lax.all_gather(a, axis), part)
    state = jax.tree.map(lambda a, e: jnp.zeros_like(a) + jnp.asarray(e, a.dtype), part, identity)

    def one(lap, state):
        return combine(
            state, jax.tree.map(lambda a: lax.dynamic_index_in_dim(a, lap, 0, False), gathered)
        )

    return lax.fori_loop(0, place, one, state)


def unit_heads(matrix, head_count, factor):
    shaped = matrix.astype(jnp.float32).reshape(matrix.shape[0], head_count, -1)
    return shaped * lax.rsqrt(jnp.sum(shaped * shaped, -1, keepdims=True) + EPSILON) * factor


def segment_of(lengths, positions):
    starts = jnp.cumsum(lengths) - lengths
    return jnp.sum((starts[:, None] <= positions[None, :]).astype(jnp.int32), 0) - 1


def block_terms(queries, key_rows, value_rows, beta_gate, decay_log, segment, seg_before):
    length = key_rows.shape[1]
    cumulative = jnp.cumsum(decay_log, axis=-1)
    rows_at = jnp.arange(length)[:, None]
    cols_at = jnp.arange(length)[None, :]
    same_doc = (segment[:, None] == segment[None, :]) & (rows_at >= cols_at)
    log_gap = jnp.minimum(cumulative[:, :, None] - cumulative[:, None, :], 0.0)
    decay_pair = jnp.where(same_doc[None], jnp.exp(log_gap), 0.0)
    from_start = jnp.where((segment == seg_before)[None, :], jnp.exp(cumulative), 0.0)
    to_end = decay_pair[:, -1, :]
    key_inner = jnp.einsum("hcd,hsd->hcs", key_rows, key_rows, precision=ROWWISE)
    lower_part = jnp.where(
        (rows_at > cols_at)[None], beta_gate[:, :, None] * decay_pair * key_inner, 0.0
    )
    system = jnp.eye(length, dtype=jnp.float32)[None] + lower_part
    right_side = jnp.concatenate(
        [beta_gate[:, :, None] * value_rows, (beta_gate * from_start)[:, :, None] * key_rows],
        axis=-1,
    )
    solved = jax.scipy.linalg.solve_triangular(system, right_side, lower=True, unit_diagonal=True)
    value_width = value_rows.shape[-1]
    pseudo = solved[..., :value_width]
    weights = solved[..., value_width:]
    scores = jnp.einsum("hcd,hsd->hcs", queries, key_rows, precision=ROWWISE) * decay_pair
    weighted = key_rows * to_end[:, :, None]
    key_width = key_rows.shape[-1]
    transition = from_start[:, -1][:, None, None] * jnp.eye(key_width, dtype=jnp.float32)[
        None
    ] - jnp.einsum("hcd,hce->hde", weighted, weights, precision=HIGHEST)
    offset = jnp.einsum("hcd,hce->hde", weighted, pseudo, precision=HIGHEST)
    return (pseudo, weights, scores, from_start, transition, offset)


def block_output(queries, pseudo, weights, scores, from_start, carried):
    errors = pseudo - jnp.einsum("hcd,hde->hce", weights, carried, precision=ROWWISE)
    return jnp.einsum(
        "hcd,hde->hce", queries * from_start[:, :, None], carried, precision=ROWWISE
    ) + jnp.einsum("hcs,hse->hce", scores, errors, precision=ROWWISE)


def apply_map(transition, carried):
    return jnp.einsum("hde,hef->hdf", transition, carried, precision=HIGHEST)


def head_blocks(matrix, block_len):
    length, head_count, inner_width = matrix.shape
    return matrix.reshape(length // block_len, block_len, head_count, inner_width).transpose(
        0, 2, 1, 3
    )


def prepare(queries, key_in, value_in, log_decay, beta_logit, segment, seg_before):
    length = queries.shape[0]
    group_size = HV // HK
    query_heads = jnp.repeat(unit_heads(queries, HK, DK ** (-0.5)), group_size, axis=1)
    key_heads = jnp.repeat(unit_heads(key_in, HK, 1.0), group_size, axis=1)
    value_heads = value_in.astype(jnp.float32).reshape(length, HV, DV)
    nblock = length // BLOCK
    beta_gate = jax.nn.sigmoid(beta_logit).reshape(HV, nblock, BLOCK).transpose(1, 0, 2)
    decay_log = log_decay.reshape(HV, nblock, BLOCK).transpose(1, 0, 2)
    seg_blocks = segment.reshape(nblock, BLOCK)
    seg_starts = jnp.concatenate([jnp.reshape(seg_before, (1,)), seg_blocks[:-1, -1]])
    query_blocks = head_blocks(query_heads, BLOCK)
    terms = jax.vmap(block_terms)(
        query_blocks,
        head_blocks(key_heads, BLOCK),
        head_blocks(value_heads, BLOCK),
        beta_gate,
        decay_log,
        seg_blocks,
        seg_starts,
    )
    return (query_blocks, terms)


def finish(query_blocks, terms, start_state, gate_in, residual_in, head_gain, out_proj):
    pseudo, weights, scores, from_start, transition, offset = terms

    def advance(carried, member):
        return (apply_map(member[0], carried) + member[1], carried)

    final_state, block_starts = lax.scan(advance, start_state, (transition, offset))
    outputs = jax.vmap(block_output)(
        query_blocks, pseudo, weights, scores, from_start, block_starts
    )
    length = gate_in.shape[0]
    outputs = outputs.transpose(0, 2, 1, 3).reshape(length, HV, DV)
    mean_square = jnp.mean(outputs * outputs, -1, keepdims=True)
    gate_heads = gate_in.astype(jnp.float32).reshape(length, HV, DV)
    normed = (
        (outputs * lax.rsqrt(mean_square + EPSILON) * head_gain * jax.nn.silu(gate_heads))
        .reshape(length, HV * DV)
        .astype(jnp.bfloat16)
    )
    mixed = jnp.dot(normed, out_proj, preferred_element_type=jnp.float32)
    return (residual_in.astype(jnp.float32) + mixed).astype(jnp.bfloat16)


def post_norm(hidden_state, post_gain):
    widened = hidden_state.astype(jnp.float32)
    return (
        widened * lax.rsqrt(jnp.mean(widened * widened, -1, keepdims=True) + EPSILON) * post_gain
    ).astype(jnp.bfloat16)


def rank_of(flat_ids, experts):
    onehot = (flat_ids[:, None] == jnp.arange(experts, dtype=jnp.int32)[None, :]).astype(jnp.int32)
    return jnp.sum((jnp.cumsum(onehot, 0) - onehot) * onehot, 1)


def expert_apply(routed, expert_in, expert_out):
    gate_up = jnp.einsum("sjcd,jdf->sjcf", routed, expert_in, preferred_element_type=jnp.float32)
    hidden_units = (jax.nn.silu(gate_up[..., :FF]) * gate_up[..., FF:]).astype(jnp.bfloat16)
    return jnp.einsum(
        "sjcf,jfd->sjcd", hidden_units, expert_out, preferred_element_type=jnp.float32
    ).astype(jnp.bfloat16)


def per_device_long(
    queries,
    key_in,
    value_in,
    gate_in,
    residual_in,
    log_decay,
    beta_logit,
    lengths,
    head_gain,
    out_proj,
    post_gain,
    expert_in,
    expert_out,
    routes,
    route_gates,
):
    tokens_dev = queries.shape[1]
    ctx_index = lax.axis_index("ctx")
    positions = ctx_index * tokens_dev + jnp.arange(tokens_dev, dtype=jnp.int32)
    segment = segment_of(lengths[0], positions)
    previous = segment_of(lengths[0], jnp.reshape(positions[0] - 1, (1,)))[0]
    seg_before = jnp.where(ctx_index > 0, previous, -1)
    query_blocks, terms = prepare(
        queries[0], key_in[0], value_in[0], log_decay[0], beta_logit[0], segment, seg_before
    )
    eye_maps = jnp.broadcast_to(jnp.eye(DK, dtype=jnp.float32), (HV, DK, DK))
    zero_offset = jnp.zeros((HV, DK, DV), jnp.float32)

    def compose(carry_pair, member):
        return (
            (apply_map(member[0], carry_pair[0]), apply_map(member[0], carry_pair[1]) + member[1]),
            None,
        )

    device_pair, unused = lax.scan(compose, (eye_maps, zero_offset), (terms[4], terms[5]))

    def combine(earlier, later):
        return (apply_map(later[0], earlier[0]), apply_map(later[0], earlier[1]) + later[1])

    prefix_map, prefix_offset = entering(
        (device_pair[0], device_pair[1]), "ctx", combine, (eye_maps, zero_offset)
    )
    hidden_state = finish(
        query_blocks, terms, prefix_offset, gate_in[0], residual_in[0], head_gain, out_proj
    )
    expert_input = post_norm(hidden_state, post_gain)
    local_experts = expert_in.shape[0]
    device_count = lax.axis_size("dp") * lax.axis_size("ctx")
    experts_all = local_experts * device_count
    capacity = tokens_dev * TOPK * 6 // (5 * experts_all)
    flat_ids = routes[0].reshape(-1)
    slot_rank = rank_of(flat_ids, experts_all)
    outbound = (
        jnp.zeros((experts_all, capacity, D), jnp.bfloat16)
        .at[flat_ids, slot_rank]
        .set(jnp.repeat(expert_input, TOPK, axis=0))
    )
    outbound = outbound.reshape(device_count, local_experts, capacity, D)
    computed = expert_apply(
        lax.all_to_all(outbound, ("dp", "ctx"), split_axis=0, concat_axis=0, tiled=True),
        expert_in,
        expert_out,
    )
    returned = lax.all_to_all(computed, ("dp", "ctx"), split_axis=0, concat_axis=0, tiled=True)
    back_rows = returned.reshape(experts_all, capacity, D)[flat_ids, slot_rank]
    expert_mix = jnp.sum(
        back_rows.astype(jnp.float32).reshape(tokens_dev, TOPK, D) * route_gates[0][:, :, None], 1
    )
    summed = hidden_state.astype(jnp.float32) + expert_mix
    return summed.astype(jnp.bfloat16)[None]


TILE = 128
SCAL = 128
BF = jnp.bfloat16
F32 = jnp.float32


def mm(a, b):
    return jnp.dot(a, b, preferred_element_type=F32)


def mm_nt(a, b):
    return lax.dot_general(a, b, (((1,), (1,)), ((), ())), preferred_element_type=F32)


def halves(a):
    high = a.astype(BF)
    return high, (a - high.astype(F32)).astype(BF)


def dot3(a, b):
    ah, al = a
    bh, bl = b
    return mm(ah, bh) + (mm(ah, bl) + mm(al, bh))


def mixer_kernel(lengths_ref, x_ref, gain_ref, out_ref, pseudo, weights, scores, keyed, ends):
    total = x_ref.shape[0]
    tiles = total // TILE
    group = HV // HK
    rows = lax.broadcasted_iota(jnp.int32, (TILE, TILE), 0)
    cols = lax.broadcasted_iota(jnp.int32, (TILE, TILE), 1)
    eye = (rows == cols).astype(F32)
    tri = (rows >= cols).astype(BF)
    starts = []
    at = jnp.int32(0)
    for j in range(lengths_ref.shape[1]):
        starts.append(at)
        at = at + lengths_ref[0, j]

    def segment(pos):
        seg = jnp.zeros(pos.shape, jnp.int32)
        for start in starts:
            seg = seg + (start <= pos).astype(jnp.int32)
        return seg

    def terms_of(tile):
        base = pl.multiple_of(tile * TILE, TILE)
        q = x_ref[pl.ds(base, TILE), 0:DK]
        k = x_ref[pl.ds(base, TILE), DK : 2 * DK]
        sc = x_ref[pl.ds(base, TILE), 2 * DK + group * DV : 2 * DK + group * DV + SCAL]
        cum = mm(tri, sc)
        qf = q.astype(F32)
        kf = k.astype(F32)
        rq = lax.rsqrt(jnp.sum(qf * qf, -1, keepdims=True) + EPSILON) * DK ** (-0.5)
        rk = lax.rsqrt(jnp.sum(kf * kf, -1, keepdims=True) + EPSILON)
        scf = sc.astype(F32)
        seg_c = segment(base + rows)
        seg_r = segment(base + cols)
        seg_b = segment(jnp.full((TILE, 1), base - 1, jnp.int32))
        causal = (seg_c == seg_r) & (rows >= cols)
        open_c = (seg_c[:, :1] == seg_b) & (base > 0)
        g_c, beta_c, from_c = [], [], []
        for h in range(group):
            g = cum[:, h : h + 1] + cum[:, group + h : group + h + 1]
            b = (
                scf[:, 2 * group + h : 2 * group + h + 1]
                + scf[:, 3 * group + h : 3 * group + h + 1]
            )
            g_c.append(g)
            beta_c.append(b)
            from_c.append(jnp.where(open_c, jnp.exp(g), 0.0))
        packed = jnp.zeros((TILE, TILE), F32)
        for n, col in enumerate(g_c + beta_c + from_c + [rk]):
            packed = jnp.where(cols == n, col, packed)
        flat = packed.T
        rk_r = flat[3 * group : 3 * group + 1, :]
        kk = mm_nt(k, k) * rk * rk_r
        qk = mm_nt(q, k) * rq * rk_r
        per_head = []
        for h in range(group):
            g_r = flat[h : h + 1, :]
            beta_r = flat[group + h : group + h + 1, :]
            from_r = flat[2 * group + h : 2 * group + h + 1, :]
            pair = jnp.where(causal, jnp.exp(jnp.minimum(g_c[h] - g_r, 0.0)), 0.0)
            lower = jnp.where(rows > cols, beta_c[h] * pair * kk, 0.0)
            last = jnp.where(
                (seg_c[TILE - 1 :, :1] == seg_c[:, :1]),
                jnp.exp(jnp.minimum(g_c[h][TILE - 1 :, :] - g_c[h], 0.0)),
                0.0,
            )
            per_head.append(
                dict(
                    tile=tile,
                    h=h,
                    base=base,
                    lower=lower,
                    score=qk * pair,
                    beta_r=beta_r,
                    scale_r=beta_r * from_r * rk_r,
                    k=k,
                    to_end=last * rk,
                    read=from_c[h] * rq,
                    from_end=from_c[h][TILE - 1 :, :],
                )
            )
        return per_head

    def build(step, carry):
        work = []
        for u in range(2):
            work += terms_of(step * 2 + u)
        near = ((rows ^ cols) == 1) & (rows > cols)
        inverse = [eye - jnp.where(near, w["lower"], 0.0) for w in work]
        level = 1
        while (1 << level) < TILE:
            mask = (((rows >> level) ^ (cols >> level)) == 1) & (rows > cols)
            parts = [halves(x) for x in inverse]
            links = [halves(jnp.where(mask, w["lower"], 0.0)) for w in work]
            first = [halves(dot3(x, c)) for x, c in zip(parts, links)]
            inverse = [x - dot3(f, p) for x, f, p in zip(inverse, first, parts)]
            level += 1
        for w, x in zip(work, inverse):
            slot = w["tile"] * group + w["h"]
            v = x_ref[
                pl.ds(w["base"], TILE), 2 * DK + w["h"] * DV : 2 * DK + (w["h"] + 1) * DV
            ]
            xh, xl = halves(x * w["beta_r"])
            pseudo[slot] = mm(xh, v) + mm(xl, v)
            wh, wl = halves(x * w["scale_r"])
            weights[slot] = mm(wh, w["k"]) + mm(wl, w["k"])
            scores[slot] = w["score"]
            keyed[slot] = jnp.where(cols == 0, w["to_end"], jnp.where(cols == 1, w["read"], 0.0))
            ends[slot] = jnp.broadcast_to(w["from_end"], (8, TILE))
        return carry

    lax.fori_loop(0, tiles // 2, build, 0)

    def advance(tile, states):
        base = pl.multiple_of(tile * TILE, TILE)
        q = x_ref[pl.ds(base, TILE), 0:DK]
        k = x_ref[pl.ds(base, TILE), DK : 2 * DK]
        following = []
        for h in range(group):
            slot = tile * group + h
            state = states[h]
            sh, sl = halves(state)
            error = pseudo[slot] - dot3(halves(weights[slot]), (sh, sl))
            scalars = keyed[slot]
            eh, el = halves(error * scalars[:, 0:1])
            grown = lax.dot_general(
                k, eh, (((0,), (0,)), ((), ())), preferred_element_type=F32
            ) + lax.dot_general(k, el, (((0,), (0,)), ((), ())), preferred_element_type=F32)
            following.append(ends[slot][0:1, :] * state + grown)
            raw = (mm(q, sh) + mm(q, sl)) * scalars[:, 1:2] + dot3(
                halves(scores[slot]), halves(error)
            )
            mean = jnp.mean(raw * raw, -1, keepdims=True)
            out_ref[pl.ds(base, TILE), h * DV : (h + 1) * DV] = (
                raw * lax.rsqrt(mean + EPSILON) * gain_ref[...]
            ).astype(BF)
        return tuple(following)

    lax.fori_loop(
        0, tiles, advance, tuple(jnp.zeros((DK, DV), F32) for h in range(group))
    )


def mixer(lengths, rows, head_gain):
    total = rows.shape[0]
    group = HV // HK
    slots = total // TILE * group
    vmem = pl.BlockSpec(memory_space=pltpu.VMEM)
    return pl.pallas_call(
        mixer_kernel,
        out_shape=jax.ShapeDtypeStruct((total, group * DV), BF),
        in_specs=[pl.BlockSpec(memory_space=pltpu.SMEM), vmem, vmem],
        out_specs=vmem,
        scratch_shapes=[
            pltpu.VMEM((slots, TILE, DV), F32),
            pltpu.VMEM((slots, TILE, DK), F32),
            pltpu.VMEM((slots, TILE, TILE), F32),
            pltpu.VMEM((slots, TILE, TILE), F32),
            pltpu.VMEM((slots, 8, TILE), F32),
        ],
        compiler_params=pltpu.CompilerParams(vmem_limit_bytes=40 * 1024 * 1024),
    )(lengths, rows, head_gain.reshape(1, DV))


def moe_kernel(
    n_dp, x_ref, hidden_ref, pick_ref, weight_ref, in_hbm, out_hbm, o_ref,
    feat, w_in, w_out, routed, units, sent, got, part, summed,
    load_sem, z_send, z_recv, d_send, d_recv, r_send, r_recv, p_send, p_recv,
):
    z = lax.axis_index("dp")
    me = lax.axis_index("ctx")
    tokens = x_ref.shape[0]
    half = tokens // 2
    rows = sent.shape[2]
    cap = rows // 2
    core, along_x, along_y = me % 2, (me // 2) % 2, me // 4

    def beside(rel):
        c = 1 - core if rel % 2 else core
        x = 1 - along_x if (rel // 2) % 2 else along_x
        y = 1 - along_y if rel // 4 else along_y
        return (z, (y * 2 + x) * 2 + c)

    far = z // 2
    inner = z + far * (3 - 2 * z)
    order = [d + far * (3 - 2 * d) for d in (inner, 1 - inner, 2, 3)]
    inward = (z + 1 - 2 * far, me)
    outward = (lax.rem(z + n_dp - 1 + 2 * far, n_dp), me)

    loads = [
        pltpu.make_async_copy(in_hbm, w_in, load_sem.at[0]),
        pltpu.make_async_copy(out_hbm, w_out, load_sem.at[1]),
    ]
    for copy in loads:
        copy.start()
    barrier = pltpu.get_barrier_semaphore()
    peers = [(lax.rem(z + s, n_dp), me) for s in range(1, n_dp)] + [beside(rel) for rel in range(1, 8)]
    for peer in peers:
        pl.semaphore_signal(barrier, inc=1, device_id=peer, device_id_type=pl.DeviceIdType.MESH)
    pl.semaphore_wait(barrier, len(peers))

    started = []

    def push(src, dst, send, recv, peer):
        copy = pltpu.make_async_remote_copy(
            src_ref=src, dst_ref=dst, send_sem=send, recv_sem=recv,
            device_id=peer, device_id_type=pl.DeviceIdType.MESH,
        )
        copy.start()
        started.append(copy)

    def arrived(dst, send, recv, peer):
        pltpu.make_async_remote_copy(
            src_ref=dst, dst_ref=dst, send_sem=send, recv_sem=recv,
            device_id=peer, device_id_type=pl.DeviceIdType.MESH,
        ).wait_recv()

    def spread(s):
        mine = feat.at[s, 0]
        push(mine, feat.at[s, 2], d_send.at[s, 0], d_recv.at[s, 0], beside(2))
        push(mine, feat.at[s, 4], d_send.at[s, 1], d_recv.at[s, 1], beside(4))
        push(mine, feat.at[s, 1], d_send.at[s, 2], d_recv.at[s, 2], beside(1))

    def forward(s):
        low, high = pl.ds(0, half), pl.ds(half, half)
        arrived(feat.at[s, 2], d_send.at[s, 0], d_recv.at[s, 0], beside(2))
        push(feat.at[s, 2, low], feat.at[s, 6, low], d_send.at[s, 3], d_recv.at[s, 3], beside(4))
        push(feat.at[s, 2], feat.at[s, 3], d_send.at[s, 5], d_recv.at[s, 5], beside(1))
        arrived(feat.at[s, 4], d_send.at[s, 1], d_recv.at[s, 1], beside(4))
        push(feat.at[s, 4, high], feat.at[s, 6, high], d_send.at[s, 4], d_recv.at[s, 4], beside(2))
        push(feat.at[s, 4], feat.at[s, 5], d_send.at[s, 6], d_recv.at[s, 6], beside(1))
        arrived(feat.at[s, 6, low], d_send.at[s, 3], d_recv.at[s, 3], beside(4))
        arrived(feat.at[s, 6, high], d_send.at[s, 4], d_recv.at[s, 4], beside(2))
        push(feat.at[s, 6], feat.at[s, 7], d_send.at[s, 7], d_recv.at[s, 7], beside(1))

    def complete(s):
        for rel, kind in ((1, 2), (3, 5), (5, 6), (7, 7)):
            arrived(feat.at[s, rel], d_send.at[s, kind], d_recv.at[s, kind], beside(1))

    def experts(s, load, between=None):
        wide = 512

        def choose(n, carry):
            at = pl.ds(pl.multiple_of(n * wide, wide), wide)
            for pair in range(4):
                block = feat[s, 2 * pair : 2 * pair + 2, :, at].reshape(2 * tokens, wide)
                found = mm(pick_ref[s, pair], block).astype(BF)
                for j in range(2):
                    routed[j, pair * rows : (pair + 1) * rows, at] = found[
                        j * rows : (j + 1) * rows
                    ]
            return carry

        lax.fori_loop(0, D // wide, choose, 0)
        if load:
            for copy in loads:
                copy.wait()
        step = 256
        for j in range(2):

            def lift(n, carry):
                lo = pl.multiple_of(n * step, step)
                g = mm(routed[j], w_in[j, :, pl.ds(lo, step)])
                u = mm(routed[j], w_in[j, :, pl.ds(lo + FF, step)])
                units[j, :, pl.ds(lo, step)] = (g / (1.0 + jnp.exp(-g)) * u).astype(BF)
                return carry

            lax.fori_loop(0, FF // step, lift, 0)

        if between is not None:
            between()

        def lower(n, carry):
            at = pl.ds(pl.multiple_of(n * wide, wide), wide)
            y = [mm(units[j], w_out[j, :, at]) for j in range(2)]
            for rel in range(8):
                block = jnp.concatenate([v[rel * cap : (rel + 1) * cap] for v in y], 0).astype(BF)
                if rel == 0:
                    got[s, 0, :, at] = block
                else:
                    sent[s, rel, :, at] = block
            return carry

        lax.fori_loop(0, D // wide, lower, 0)
        for rel in (6, 7, 2, 4, 3, 5, 1):
            push(sent.at[s, rel], got.at[s, rel], r_send.at[s, rel], r_recv.at[s, rel], beside(rel))

    def combine(s, remote):
        for rel in range(1, 8):
            arrived(got.at[s, rel], r_send.at[s, rel], r_recv.at[s, rel], beside(rel))
        wide = 512

        def mix(n, carry):
            at = pl.ds(pl.multiple_of(n * wide, wide), wide)
            part[s, :, at] = mm(
                weight_ref[s], got[s, :, :, at].reshape(8 * rows, wide)
            ).astype(BF)
            return carry

        lax.fori_loop(0, D // wide, mix, 0)
        if remote:
            push(part.at[s], summed.at[z], p_send.at[s], p_recv.at[z], (s, me))

    def along(place, slot, peer):
        d = order[place]
        return pltpu.make_async_remote_copy(
            src_ref=feat.at[d, 0], dst_ref=feat.at[d, 0], send_sem=z_send.at[slot],
            recv_sem=z_recv.at[d], device_id=peer, device_id_type=pl.DeviceIdType.MESH,
        )

    def take(place):
        d = order[place]
        along(place, 0, inward).wait_recv()

        @pl.when(inner == 1)
        def pass_on():
            along(place, place + 1, inward if place == 1 else outward).start()

    own, first, second, third = order
    feat[own, 0] = x_ref[...]
    along(0, 0, inward).start()

    @pl.when(inner == 1)
    def both_ways():
        along(0, 1, outward).start()

    spread(own)
    take(1)
    spread(first)
    forward(own)
    take(2)
    forward(first)
    spread(second)
    take(3)
    complete(first)

    def during_first():
        spread(third)
        forward(second)

    experts(first, True, during_first)
    complete(second)
    experts(second, False, lambda: forward(third))
    complete(third)
    experts(third, False)
    combine(first, True)
    complete(own)
    experts(own, False)
    combine(second, True)
    combine(third, True)
    combine(own, False)
    total = hidden_ref[...].astype(F32) + part[own].astype(F32)
    for d in (first, second, third):
        arrived(summed.at[d], p_send.at[d], p_recv.at[d], (d, me))
        total = total + summed[d].astype(F32)
    o_ref[...] = total.astype(BF)
    along(0, 0, inward).wait_send()

    @pl.when(inner == 1)
    def passed():
        along(0, 1, outward).wait_send()
        for place in range(1, n_dp):
            along(place, place + 1, inward if place == 1 else outward).wait_send()

    for copy in started:
        copy.wait_send()


def moe(n_dp, expert_input, hidden_state, pick, weight, expert_in, expert_out):
    tokens = expert_input.shape[0]
    rows = pick.shape[2] // 2
    vmem = pl.BlockSpec(memory_space=pltpu.VMEM)
    hbm = pl.BlockSpec(memory_space=pl.ANY)
    dma = pltpu.SemaphoreType.DMA
    return pl.pallas_call(
        functools.partial(moe_kernel, n_dp),
        out_shape=jax.ShapeDtypeStruct((tokens, D), BF),
        in_specs=[vmem, vmem, vmem, vmem, hbm, hbm],
        out_specs=vmem,
        scratch_shapes=[
            pltpu.VMEM((n_dp, 8, tokens, D), BF),
            pltpu.VMEM(expert_in.shape, BF),
            pltpu.VMEM(expert_out.shape, BF),
            pltpu.VMEM((2, 4 * rows, D), BF),
            pltpu.VMEM((2, 4 * rows, FF), BF),
            pltpu.VMEM((n_dp, 8, rows, D), BF),
            pltpu.VMEM((n_dp, 8, rows, D), BF),
            pltpu.VMEM((n_dp, tokens, D), BF),
            pltpu.VMEM((n_dp, tokens, D), BF),
            dma((2,)),
            dma((n_dp + 1,)),
            dma((n_dp,)),
            dma((n_dp, 8)),
            dma((n_dp, 8)),
            dma((n_dp, 8)),
            dma((n_dp, 8)),
            dma((n_dp,)),
            dma((n_dp,)),
        ],
        compiler_params=pltpu.CompilerParams(
            collective_id=0, has_side_effects=True, vmem_limit_bytes=60 * 1024 * 1024
        ),
    )(expert_input, hidden_state, pick, weight, expert_in, expert_out)


def two_parts(a):
    high = lax.reduce_precision(a, 8, 7)
    return high.astype(BF), (a - high).astype(BF)


def slot_table(gate_rows, capacity):
    named = gate_rows > 0.0
    tokens = gate_rows.shape[-1]
    before = (
        jnp.arange(tokens, dtype=jnp.int32)[:, None] < jnp.arange(tokens, dtype=jnp.int32)[None, :]
    ).astype(BF)
    rank = jnp.einsum("...t,tu->...u", named.astype(BF), before, preferred_element_type=F32)
    slot = jnp.arange(capacity, dtype=jnp.int32).astype(F32)
    return named[..., None, :] & (rank[..., None, :] == slot[:, None])


def per_device(
    queries,
    key_in,
    value_in,
    gate_in,
    residual_in,
    log_decay,
    beta_logit,
    lengths,
    head_gain,
    out_proj,
    post_gain,
    expert_in,
    expert_out,
    routes,
    route_gates,
):
    tokens = queries.shape[1]
    n_ctx = lax.axis_size("ctx")
    n_dp = lax.axis_size("dp")
    local = expert_in.shape[0]
    devices = n_ctx * n_dp
    experts = local * devices
    capacity = tokens * TOPK * 6 // (5 * experts)
    group = HV // HK
    my_dp = lax.axis_index("dp")
    my_ctx = lax.axis_index("ctx")

    ids = jnp.arange(experts, dtype=jnp.int32)[:, None]
    gate_table = jnp.zeros((experts, tokens), F32)
    for k in range(TOPK):
        gate_table = gate_table + jnp.where(
            routes[0, :, k][None, :] == ids, route_gates[0, :, k][None, :], 0.0
        )
    gate_table = gate_table.astype(BF)
    column_gates = lax.all_gather(gate_table, "dp")
    gate_cols = gate_table.reshape(n_dp, n_ctx, local, tokens).transpose(1, 3, 0, 2)
    gate_cols = gate_cols.reshape(n_ctx, tokens, n_dp * local)

    beta = jax.nn.sigmoid(beta_logit[0])
    dh, dl = two_parts(log_decay[0])
    bh, bl = two_parts(beta)
    scal = jnp.stack([dh, dl, bh, bl]).reshape(4, n_ctx, group, tokens)
    scal = scal.transpose(1, 3, 0, 2).reshape(n_ctx, tokens, 4 * group)
    scal = jnp.concatenate([scal, gate_cols], -1)
    scal = jnp.pad(scal, ((0, 0), (0, 0), (0, SCAL - scal.shape[-1])))

    def by_head(a):
        return a[0].reshape(tokens, n_ctx, -1).transpose(1, 0, 2)

    sent = jnp.concatenate([by_head(queries), by_head(key_in), by_head(value_in), scal], -1)
    heads = lax.all_to_all(sent, "ctx", split_axis=0, concat_axis=0, tiled=True)
    gates_at = 2 * DK + group * DV + 4 * group
    plane_gates = lax.all_gather(heads[:, :, gates_at : gates_at + n_dp * local], "dp")
    mixed = mixer(lengths, heads.reshape(n_ctx * tokens, -1), head_gain)
    mine = lax.all_to_all(
        mixed.reshape(n_ctx, tokens, group * DV), "ctx", split_axis=0, concat_axis=0, tiled=True
    )
    unit = mine.transpose(1, 0, 2).reshape(tokens, HV * DV)
    normed = (unit.astype(F32) * jax.nn.silu(gate_in[0].astype(F32))).astype(BF)
    projected = jnp.dot(normed, out_proj, preferred_element_type=F32)
    hidden_state = (residual_in[0].astype(F32) + projected).astype(BF)
    expert_input = post_norm(hidden_state, post_gain)

    places = my_ctx ^ jnp.arange(n_ctx)
    my_gates = plane_gates.reshape(n_dp, n_ctx, tokens, n_dp, local)
    my_gates = lax.dynamic_index_in_dim(my_gates, my_dp, 3, False).transpose(0, 1, 3, 2)
    my_gates = my_gates[:, places]
    pick = slot_table(my_gates, capacity).astype(BF)
    pick = pick.reshape(n_dp, n_ctx // 2, 2, local, capacity, tokens).transpose(0, 1, 3, 2, 4, 5)
    pick = pick[..., None, :] * jnp.eye(2, dtype=BF)[:, None, :, None]
    pick = pick.reshape(n_dp, n_ctx // 2, local * 2 * capacity, 2 * tokens)
    plane = column_gates.reshape(n_dp, n_dp, n_ctx, local, tokens)
    plane = lax.dynamic_index_in_dim(plane, my_dp, 1, False)[:, places]
    weight = jnp.where(slot_table(plane, capacity), plane[..., None, :], 0)
    weight = weight.reshape(n_dp, n_ctx * local * capacity, tokens).transpose(0, 2, 1)
    return moe(n_dp, expert_input, hidden_state, pick, weight, expert_in, expert_out)[None]


def solution(mesh):
    in_specs = (
        P("dp", "ctx", None),
        P("dp", "ctx", None),
        P("dp", "ctx", None),
        P("dp", "ctx", None),
        P("dp", "ctx", None),
        P("dp", None, "ctx"),
        P("dp", None, "ctx"),
        P("dp", None),
        P(),
        P(),
        P(),
        P(("dp", "ctx"), None, None),
        P(("dp", "ctx"), None, None),
        P("dp", "ctx", None),
        P("dp", "ctx", None),
    )
    out_specs = P("dp", "ctx", None)
    by_heads = mesh.shape["ctx"] == HK and mesh.shape["dp"] == 4
    return jax.shard_map(
        per_device if by_heads else per_device_long, mesh=mesh, in_specs=in_specs, out_specs=out_specs, check_vma=False
    )
```

```python
import functools

import jax
import jax.numpy as jnp
from jax import lax
from jax.experimental import pallas as pl
from jax.experimental.pallas import tpu as pltpu
from jax.sharding import PartitionSpec as P

D = 2048
DK = 128
DV = 128
FF = 512
TOPK = 10
HK = 8
HV = 16
BLOCK = 64


EPSILON = 1e-06
HIGHEST = lax.Precision.HIGHEST
ROWWISE = lax.Precision.HIGH


def entering(part, axis, combine, identity):
    place = lax.axis_index(axis)
    gathered = jax.tree.map(lambda a: lax.all_gather(a, axis), part)
    state = jax.tree.map(lambda a, e: jnp.zeros_like(a) + jnp.asarray(e, a.dtype), part, identity)

    def one(lap, state):
        return combine(
            state, jax.tree.map(lambda a: lax.dynamic_index_in_dim(a, lap, 0, False), gathered)
        )

    return lax.fori_loop(0, place, one, state)


def unit_heads(matrix, head_count, factor):
    shaped = matrix.astype(jnp.float32).reshape(matrix.shape[0], head_count, -1)
    return shaped * lax.rsqrt(jnp.sum(shaped * shaped, -1, keepdims=True) + EPSILON) * factor


def segment_of(lengths, positions):
    starts = jnp.cumsum(lengths) - lengths
    return jnp.sum((starts[:, None] <= positions[None, :]).astype(jnp.int32), 0) - 1


def block_terms(queries, key_rows, value_rows, beta_gate, decay_log, segment, seg_before):
    length = key_rows.shape[1]
    cumulative = jnp.cumsum(decay_log, axis=-1)
    rows_at = jnp.arange(length)[:, None]
    cols_at = jnp.arange(length)[None, :]
    same_doc = (segment[:, None] == segment[None, :]) & (rows_at >= cols_at)
    log_gap = jnp.minimum(cumulative[:, :, None] - cumulative[:, None, :], 0.0)
    decay_pair = jnp.where(same_doc[None], jnp.exp(log_gap), 0.0)
    from_start = jnp.where((segment == seg_before)[None, :], jnp.exp(cumulative), 0.0)
    to_end = decay_pair[:, -1, :]
    key_inner = jnp.einsum("hcd,hsd->hcs", key_rows, key_rows, precision=ROWWISE)
    lower_part = jnp.where(
        (rows_at > cols_at)[None], beta_gate[:, :, None] * decay_pair * key_inner, 0.0
    )
    system = jnp.eye(length, dtype=jnp.float32)[None] + lower_part
    right_side = jnp.concatenate(
        [beta_gate[:, :, None] * value_rows, (beta_gate * from_start)[:, :, None] * key_rows],
        axis=-1,
    )
    solved = jax.scipy.linalg.solve_triangular(system, right_side, lower=True, unit_diagonal=True)
    value_width = value_rows.shape[-1]
    pseudo = solved[..., :value_width]
    weights = solved[..., value_width:]
    scores = jnp.einsum("hcd,hsd->hcs", queries, key_rows, precision=ROWWISE) * decay_pair
    weighted = key_rows * to_end[:, :, None]
    key_width = key_rows.shape[-1]
    transition = from_start[:, -1][:, None, None] * jnp.eye(key_width, dtype=jnp.float32)[
        None
    ] - jnp.einsum("hcd,hce->hde", weighted, weights, precision=HIGHEST)
    offset = jnp.einsum("hcd,hce->hde", weighted, pseudo, precision=HIGHEST)
    return (pseudo, weights, scores, from_start, transition, offset)


def block_output(queries, pseudo, weights, scores, from_start, carried):
    errors = pseudo - jnp.einsum("hcd,hde->hce", weights, carried, precision=ROWWISE)
    return jnp.einsum(
        "hcd,hde->hce", queries * from_start[:, :, None], carried, precision=ROWWISE
    ) + jnp.einsum("hcs,hse->hce", scores, errors, precision=ROWWISE)


def apply_map(transition, carried):
    return jnp.einsum("hde,hef->hdf", transition, carried, precision=HIGHEST)


def head_blocks(matrix, block_len):
    length, head_count, inner_width = matrix.shape
    return matrix.reshape(length // block_len, block_len, head_count, inner_width).transpose(
        0, 2, 1, 3
    )


def prepare(queries, key_in, value_in, log_decay, beta_logit, segment, seg_before):
    length = queries.shape[0]
    group_size = HV // HK
    query_heads = jnp.repeat(unit_heads(queries, HK, DK ** (-0.5)), group_size, axis=1)
    key_heads = jnp.repeat(unit_heads(key_in, HK, 1.0), group_size, axis=1)
    value_heads = value_in.astype(jnp.float32).reshape(length, HV, DV)
    nblock = length // BLOCK
    beta_gate = jax.nn.sigmoid(beta_logit).reshape(HV, nblock, BLOCK).transpose(1, 0, 2)
    decay_log = log_decay.reshape(HV, nblock, BLOCK).transpose(1, 0, 2)
    seg_blocks = segment.reshape(nblock, BLOCK)
    seg_starts = jnp.concatenate([jnp.reshape(seg_before, (1,)), seg_blocks[:-1, -1]])
    query_blocks = head_blocks(query_heads, BLOCK)
    terms = jax.vmap(block_terms)(
        query_blocks,
        head_blocks(key_heads, BLOCK),
        head_blocks(value_heads, BLOCK),
        beta_gate,
        decay_log,
        seg_blocks,
        seg_starts,
    )
    return (query_blocks, terms)


def finish(query_blocks, terms, start_state, gate_in, residual_in, head_gain, out_proj):
    pseudo, weights, scores, from_start, transition, offset = terms

    def advance(carried, member):
        return (apply_map(member[0], carried) + member[1], carried)

    final_state, block_starts = lax.scan(advance, start_state, (transition, offset))
    outputs = jax.vmap(block_output)(
        query_blocks, pseudo, weights, scores, from_start, block_starts
    )
    length = gate_in.shape[0]
    outputs = outputs.transpose(0, 2, 1, 3).reshape(length, HV, DV)
    mean_square = jnp.mean(outputs * outputs, -1, keepdims=True)
    gate_heads = gate_in.astype(jnp.float32).reshape(length, HV, DV)
    normed = (
        (outputs * lax.rsqrt(mean_square + EPSILON) * head_gain * jax.nn.silu(gate_heads))
        .reshape(length, HV * DV)
        .astype(jnp.bfloat16)
    )
    mixed = jnp.dot(normed, out_proj, preferred_element_type=jnp.float32)
    return (residual_in.astype(jnp.float32) + mixed).astype(jnp.bfloat16)


def post_norm(hidden_state, post_gain):
    widened = hidden_state.astype(jnp.float32)
    return (
        widened * lax.rsqrt(jnp.mean(widened * widened, -1, keepdims=True) + EPSILON) * post_gain
    ).astype(jnp.bfloat16)


def rank_of(flat_ids, experts):
    onehot = (flat_ids[:, None] == jnp.arange(experts, dtype=jnp.int32)[None, :]).astype(jnp.int32)
    return jnp.sum((jnp.cumsum(onehot, 0) - onehot) * onehot, 1)


def expert_apply(routed, expert_in, expert_out):
    gate_up = jnp.einsum("sjcd,jdf->sjcf", routed, expert_in, preferred_element_type=jnp.float32)
    hidden_units = (jax.nn.silu(gate_up[..., :FF]) * gate_up[..., FF:]).astype(jnp.bfloat16)
    return jnp.einsum(
        "sjcf,jfd->sjcd", hidden_units, expert_out, preferred_element_type=jnp.float32
    ).astype(jnp.bfloat16)


def per_device_long(
    queries,
    key_in,
    value_in,
    gate_in,
    residual_in,
    log_decay,
    beta_logit,
    lengths,
    head_gain,
    out_proj,
    post_gain,
    expert_in,
    expert_out,
    routes,
    route_gates,
):
    tokens_dev = queries.shape[1]
    ctx_index = lax.axis_index("ctx")
    positions = ctx_index * tokens_dev + jnp.arange(tokens_dev, dtype=jnp.int32)
    segment = segment_of(lengths[0], positions)
    previous = segment_of(lengths[0], jnp.reshape(positions[0] - 1, (1,)))[0]
    seg_before = jnp.where(ctx_index > 0, previous, -1)
    query_blocks, terms = prepare(
        queries[0], key_in[0], value_in[0], log_decay[0], beta_logit[0], segment, seg_before
    )
    eye_maps = jnp.broadcast_to(jnp.eye(DK, dtype=jnp.float32), (HV, DK, DK))
    zero_offset = jnp.zeros((HV, DK, DV), jnp.float32)

    def compose(carry_pair, member):
        return (
            (apply_map(member[0], carry_pair[0]), apply_map(member[0], carry_pair[1]) + member[1]),
            None,
        )

    device_pair, unused = lax.scan(compose, (eye_maps, zero_offset), (terms[4], terms[5]))

    def combine(earlier, later):
        return (apply_map(later[0], earlier[0]), apply_map(later[0], earlier[1]) + later[1])

    prefix_map, prefix_offset = entering(
        (device_pair[0], device_pair[1]), "ctx", combine, (eye_maps, zero_offset)
    )
    hidden_state = finish(
        query_blocks, terms, prefix_offset, gate_in[0], residual_in[0], head_gain, out_proj
    )
    expert_input = post_norm(hidden_state, post_gain)
    local_experts = expert_in.shape[0]
    device_count = lax.axis_size("dp") * lax.axis_size("ctx")
    experts_all = local_experts * device_count
    capacity = tokens_dev * TOPK * 6 // (5 * experts_all)
    flat_ids = routes[0].reshape(-1)
    slot_rank = rank_of(flat_ids, experts_all)
    outbound = (
        jnp.zeros((experts_all, capacity, D), jnp.bfloat16)
        .at[flat_ids, slot_rank]
        .set(jnp.repeat(expert_input, TOPK, axis=0))
    )
    outbound = outbound.reshape(device_count, local_experts, capacity, D)
    computed = expert_apply(
        lax.all_to_all(outbound, ("dp", "ctx"), split_axis=0, concat_axis=0, tiled=True),
        expert_in,
        expert_out,
    )
    returned = lax.all_to_all(computed, ("dp", "ctx"), split_axis=0, concat_axis=0, tiled=True)
    back_rows = returned.reshape(experts_all, capacity, D)[flat_ids, slot_rank]
    expert_mix = jnp.sum(
        back_rows.astype(jnp.float32).reshape(tokens_dev, TOPK, D) * route_gates[0][:, :, None], 1
    )
    summed = hidden_state.astype(jnp.float32) + expert_mix
    return summed.astype(jnp.bfloat16)[None]


TILE = 128
SCAL = 128
BF = jnp.bfloat16
F32 = jnp.float32


def mm(a, b):
    return jnp.dot(a, b, preferred_element_type=F32)


def mm_nt(a, b):
    return lax.dot_general(a, b, (((1,), (1,)), ((), ())), preferred_element_type=F32)


def halves(a):
    high = a.astype(BF)
    return high, (a - high.astype(F32)).astype(BF)


def dot3(a, b):
    ah, al = a
    bh, bl = b
    return mm(ah, bh) + (mm(ah, bl) + mm(al, bh))


def mixer_kernel(lengths_ref, x_ref, gain_ref, out_ref, pseudo, weights, scores, keyed, ends):
    total = x_ref.shape[0]
    tiles = total // TILE
    group = HV // HK
    rows = lax.broadcasted_iota(jnp.int32, (TILE, TILE), 0)
    cols = lax.broadcasted_iota(jnp.int32, (TILE, TILE), 1)
    eye = (rows == cols).astype(F32)
    tri = (rows >= cols).astype(BF)
    starts = []
    at = jnp.int32(0)
    for j in range(lengths_ref.shape[1]):
        starts.append(at)
        at = at + lengths_ref[0, j]

    def segment(pos):
        seg = jnp.zeros(pos.shape, jnp.int32)
        for start in starts:
            seg = seg + (start <= pos).astype(jnp.int32)
        return seg

    def terms_of(tile):
        base = pl.multiple_of(tile * TILE, TILE)
        q = x_ref[pl.ds(base, TILE), 0:DK]
        k = x_ref[pl.ds(base, TILE), DK : 2 * DK]
        sc = x_ref[pl.ds(base, TILE), 2 * DK + group * DV : 2 * DK + group * DV + SCAL]
        cum = mm(tri, sc)
        qf = q.astype(F32)
        kf = k.astype(F32)
        rq = lax.rsqrt(jnp.sum(qf * qf, -1, keepdims=True) + EPSILON) * DK ** (-0.5)
        rk = lax.rsqrt(jnp.sum(kf * kf, -1, keepdims=True) + EPSILON)
        scf = sc.astype(F32)
        seg_c = segment(base + rows)
        seg_r = segment(base + cols)
        seg_b = segment(jnp.full((TILE, 1), base - 1, jnp.int32))
        causal = (seg_c == seg_r) & (rows >= cols)
        open_c = (seg_c[:, :1] == seg_b) & (base > 0)
        g_c, beta_c, from_c = [], [], []
        for h in range(group):
            g = cum[:, h : h + 1] + cum[:, group + h : group + h + 1]
            b = (
                scf[:, 2 * group + h : 2 * group + h + 1]
                + scf[:, 3 * group + h : 3 * group + h + 1]
            )
            g_c.append(g)
            beta_c.append(b)
            from_c.append(jnp.where(open_c, jnp.exp(g), 0.0))
        packed = jnp.zeros((TILE, TILE), F32)
        for n, col in enumerate(g_c + beta_c + from_c + [rk]):
            packed = jnp.where(cols == n, col, packed)
        flat = packed.T
        rk_r = flat[3 * group : 3 * group + 1, :]
        kk = mm_nt(k, k) * rk * rk_r
        qk = mm_nt(q, k) * rq * rk_r
        per_head = []
        for h in range(group):
            g_r = flat[h : h + 1, :]
            beta_r = flat[group + h : group + h + 1, :]
            from_r = flat[2 * group + h : 2 * group + h + 1, :]
            pair = jnp.where(causal, jnp.exp(jnp.minimum(g_c[h] - g_r, 0.0)), 0.0)
            lower = jnp.where(rows > cols, beta_c[h] * pair * kk, 0.0)
            last = jnp.where(
                (seg_c[TILE - 1 :, :1] == seg_c[:, :1]),
                jnp.exp(jnp.minimum(g_c[h][TILE - 1 :, :] - g_c[h], 0.0)),
                0.0,
            )
            per_head.append(
                dict(
                    tile=tile,
                    h=h,
                    base=base,
                    lower=lower,
                    score=qk * pair,
                    beta_r=beta_r,
                    scale_r=beta_r * from_r * rk_r,
                    k=k,
                    to_end=last * rk,
                    read=from_c[h] * rq,
                    from_end=from_c[h][TILE - 1 :, :],
                )
            )
        return per_head

    def build(step, carry):
        work = []
        for u in range(2):
            work += terms_of(step * 2 + u)
        near = ((rows ^ cols) == 1) & (rows > cols)
        inverse = [eye - jnp.where(near, w["lower"], 0.0) for w in work]
        level = 1
        while (1 << level) < TILE:
            mask = (((rows >> level) ^ (cols >> level)) == 1) & (rows > cols)
            parts = [halves(x) for x in inverse]
            links = [halves(jnp.where(mask, w["lower"], 0.0)) for w in work]
            first = [halves(dot3(x, c)) for x, c in zip(parts, links)]
            inverse = [x - dot3(f, p) for x, f, p in zip(inverse, first, parts)]
            level += 1
        for w, x in zip(work, inverse):
            slot = w["tile"] * group + w["h"]
            v = x_ref[
                pl.ds(w["base"], TILE), 2 * DK + w["h"] * DV : 2 * DK + (w["h"] + 1) * DV
            ]
            xh, xl = halves(x * w["beta_r"])
            pseudo[slot] = mm(xh, v) + mm(xl, v)
            wh, wl = halves(x * w["scale_r"])
            weights[slot] = mm(wh, w["k"]) + mm(wl, w["k"])
            scores[slot] = w["score"]
            keyed[slot] = jnp.where(cols == 0, w["to_end"], jnp.where(cols == 1, w["read"], 0.0))
            ends[slot] = jnp.broadcast_to(w["from_end"], (8, TILE))
        return carry

    lax.fori_loop(0, tiles // 2, build, 0)

    def advance(tile, states):
        base = pl.multiple_of(tile * TILE, TILE)
        q = x_ref[pl.ds(base, TILE), 0:DK]
        k = x_ref[pl.ds(base, TILE), DK : 2 * DK]
        following = []
        for h in range(group):
            slot = tile * group + h
            state = states[h]
            sh, sl = halves(state)
            error = pseudo[slot] - dot3(halves(weights[slot]), (sh, sl))
            scalars = keyed[slot]
            eh, el = halves(error * scalars[:, 0:1])
            grown = lax.dot_general(
                k, eh, (((0,), (0,)), ((), ())), preferred_element_type=F32
            ) + lax.dot_general(k, el, (((0,), (0,)), ((), ())), preferred_element_type=F32)
            following.append(ends[slot][0:1, :] * state + grown)
            raw = (mm(q, sh) + mm(q, sl)) * scalars[:, 1:2] + dot3(
                halves(scores[slot]), halves(error)
            )
            mean = jnp.mean(raw * raw, -1, keepdims=True)
            out_ref[pl.ds(base, TILE), h * DV : (h + 1) * DV] = (
                raw * lax.rsqrt(mean + EPSILON) * gain_ref[...]
            ).astype(BF)
        return tuple(following)

    lax.fori_loop(
        0, tiles, advance, tuple(jnp.zeros((DK, DV), F32) for h in range(group))
    )


def mixer(lengths, rows, head_gain):
    total = rows.shape[0]
    group = HV // HK
    slots = total // TILE * group
    vmem = pl.BlockSpec(memory_space=pltpu.VMEM)
    return pl.pallas_call(
        mixer_kernel,
        out_shape=jax.ShapeDtypeStruct((total, group * DV), BF),
        in_specs=[pl.BlockSpec(memory_space=pltpu.SMEM), vmem, vmem],
        out_specs=vmem,
        scratch_shapes=[
            pltpu.VMEM((slots, TILE, DV), F32),
            pltpu.VMEM((slots, TILE, DK), F32),
            pltpu.VMEM((slots, TILE, TILE), F32),
            pltpu.VMEM((slots, TILE, TILE), F32),
            pltpu.VMEM((slots, 8, TILE), F32),
        ],
        compiler_params=pltpu.CompilerParams(vmem_limit_bytes=40 * 1024 * 1024),
    )(lengths, rows, head_gain.reshape(1, DV))


def moe_kernel(
    n_dp, x_ref, hidden_ref, pick_ref, weight_ref, in_hbm, out_hbm, o_ref,
    feat, w_in, w_out, routed, units, sent, got, part, summed,
    load_sem, z_send, z_recv, d_send, d_recv, r_send, r_recv, p_send, p_recv,
):
    z = lax.axis_index("dp")
    me = lax.axis_index("ctx")
    tokens = x_ref.shape[0]
    half = tokens // 2
    rows = sent.shape[2]
    cap = rows // 2
    core, along_x, along_y = me % 2, (me // 2) % 2, me // 4

    def beside(rel):
        c = 1 - core if rel % 2 else core
        x = 1 - along_x if (rel // 2) % 2 else along_x
        y = 1 - along_y if rel // 4 else along_y
        return (z, (y * 2 + x) * 2 + c)

    far = z // 2
    inner = z + far * (3 - 2 * z)
    order = [d + far * (3 - 2 * d) for d in (inner, 1 - inner, 2, 3)]
    inward = (z + 1 - 2 * far, me)
    outward = (lax.rem(z + n_dp - 1 + 2 * far, n_dp), me)

    loads = [
        pltpu.make_async_copy(in_hbm, w_in, load_sem.at[0]),
        pltpu.make_async_copy(out_hbm, w_out, load_sem.at[1]),
    ]
    for copy in loads:
        copy.start()
    barrier = pltpu.get_barrier_semaphore()
    peers = [(lax.rem(z + s, n_dp), me) for s in range(1, n_dp)] + [beside(rel) for rel in range(1, 8)]
    for peer in peers:
        pl.semaphore_signal(barrier, inc=1, device_id=peer, device_id_type=pl.DeviceIdType.MESH)
    pl.semaphore_wait(barrier, len(peers))

    started = []

    def push(src, dst, send, recv, peer):
        copy = pltpu.make_async_remote_copy(
            src_ref=src, dst_ref=dst, send_sem=send, recv_sem=recv,
            device_id=peer, device_id_type=pl.DeviceIdType.MESH,
        )
        copy.start()
        started.append(copy)

    def arrived(dst, send, recv, peer):
        pltpu.make_async_remote_copy(
            src_ref=dst, dst_ref=dst, send_sem=send, recv_sem=recv,
            device_id=peer, device_id_type=pl.DeviceIdType.MESH,
        ).wait_recv()

    def spread(s):
        mine = feat.at[s, 0]
        push(mine, feat.at[s, 2], d_send.at[s, 0], d_recv.at[s, 0], beside(2))
        push(mine, feat.at[s, 4], d_send.at[s, 1], d_recv.at[s, 1], beside(4))
        push(mine, feat.at[s, 1], d_send.at[s, 2], d_recv.at[s, 2], beside(1))

    def forward(s):
        low, high = pl.ds(0, half), pl.ds(half, half)
        arrived(feat.at[s, 2], d_send.at[s, 0], d_recv.at[s, 0], beside(2))
        push(feat.at[s, 2, low], feat.at[s, 6, low], d_send.at[s, 3], d_recv.at[s, 3], beside(4))
        push(feat.at[s, 2], feat.at[s, 3], d_send.at[s, 5], d_recv.at[s, 5], beside(1))
        arrived(feat.at[s, 4], d_send.at[s, 1], d_recv.at[s, 1], beside(4))
        push(feat.at[s, 4, high], feat.at[s, 6, high], d_send.at[s, 4], d_recv.at[s, 4], beside(2))
        push(feat.at[s, 4], feat.at[s, 5], d_send.at[s, 6], d_recv.at[s, 6], beside(1))
        arrived(feat.at[s, 6, low], d_send.at[s, 3], d_recv.at[s, 3], beside(4))
        arrived(feat.at[s, 6, high], d_send.at[s, 4], d_recv.at[s, 4], beside(2))
        push(feat.at[s, 6], feat.at[s, 7], d_send.at[s, 7], d_recv.at[s, 7], beside(1))

    def complete(s):
        for rel, kind in ((1, 2), (3, 5), (5, 6), (7, 7)):
            arrived(feat.at[s, rel], d_send.at[s, kind], d_recv.at[s, kind], beside(1))

    def experts(s, load, between=None):
        wide = 512

        def choose(n, carry):
            at = pl.ds(pl.multiple_of(n * wide, wide), wide)
            for pair in range(4):
                block = feat[s, 2 * pair : 2 * pair + 2, :, at].reshape(2 * tokens, wide)
                found = mm(pick_ref[s, pair], block).astype(BF)
                for j in range(2):
                    routed[j, pair * rows : (pair + 1) * rows, at] = found[
                        j * rows : (j + 1) * rows
                    ]
            return carry

        lax.fori_loop(0, D // wide, choose, 0)
        if load:
            for copy in loads:
                copy.wait()
        step = 256
        for j in range(2):

            def lift(n, carry):
                lo = pl.multiple_of(n * step, step)
                g = mm(routed[j], w_in[j, :, pl.ds(lo, step)])
                u = mm(routed[j], w_in[j, :, pl.ds(lo + FF, step)])
                units[j, :, pl.ds(lo, step)] = (g / (1.0 + jnp.exp(-g)) * u).astype(BF)
                return carry

            lax.fori_loop(0, FF // step, lift, 0)

        if between is not None:
            between()

        def lower(n, carry):
            at = pl.ds(pl.multiple_of(n * wide, wide), wide)
            y = [mm(units[j], w_out[j, :, at]) for j in range(2)]
            for rel in range(8):
                block = jnp.concatenate([v[rel * cap : (rel + 1) * cap] for v in y], 0).astype(BF)
                if rel == 0:
                    got[s, 0, :, at] = block
                else:
                    sent[s, rel, :, at] = block
            return carry

        lax.fori_loop(0, D // wide, lower, 0)
        for rel in (6, 7, 2, 4, 3, 5, 1):
            push(sent.at[s, rel], got.at[s, rel], r_send.at[s, rel], r_recv.at[s, rel], beside(rel))

    def combine(s, remote):
        for rel in range(1, 8):
            arrived(got.at[s, rel], r_send.at[s, rel], r_recv.at[s, rel], beside(rel))
        wide = 512

        def mix(n, carry):
            at = pl.ds(pl.multiple_of(n * wide, wide), wide)
            part[s, :, at] = mm(
                weight_ref[s], got[s, :, :, at].reshape(8 * rows, wide)
            ).astype(BF)
            return carry

        lax.fori_loop(0, D // wide, mix, 0)
        if remote:
            push(part.at[s], summed.at[z], p_send.at[s], p_recv.at[z], (s, me))

    def along(place, slot, peer):
        d = order[place]
        return pltpu.make_async_remote_copy(
            src_ref=feat.at[d, 0], dst_ref=feat.at[d, 0], send_sem=z_send.at[slot],
            recv_sem=z_recv.at[d], device_id=peer, device_id_type=pl.DeviceIdType.MESH,
        )

    def take(place):
        d = order[place]
        along(place, 0, inward).wait_recv()

        @pl.when(inner == 1)
        def pass_on():
            along(place, place + 1, inward if place == 1 else outward).start()

    own, first, second, third = order
    feat[own, 0] = x_ref[...]
    along(0, 0, inward).start()

    @pl.when(inner == 1)
    def both_ways():
        along(0, 1, outward).start()

    spread(own)
    take(1)
    spread(first)
    forward(own)
    take(2)
    forward(first)
    spread(second)
    take(3)
    complete(first)

    def during_first():
        spread(third)
        forward(second)

    experts(first, True, during_first)
    complete(second)
    experts(second, False, lambda: forward(third))
    complete(third)
    experts(third, False)
    combine(first, True)
    complete(own)
    experts(own, False)
    combine(second, True)
    combine(third, True)
    combine(own, False)
    total = hidden_ref[...].astype(F32) + part[own].astype(F32)
    for d in (first, second, third):
        arrived(summed.at[d], p_send.at[d], p_recv.at[d], (d, me))
        total = total + summed[d].astype(F32)
    o_ref[...] = total.astype(BF)
    along(0, 0, inward).wait_send()

    @pl.when(inner == 1)
    def passed():
        along(0, 1, outward).wait_send()
        for place in range(1, n_dp):
            along(place, place + 1, inward if place == 1 else outward).wait_send()

    for copy in started:
        copy.wait_send()


def moe(n_dp, expert_input, hidden_state, pick, weight, expert_in, expert_out):
    tokens = expert_input.shape[0]
    rows = pick.shape[2] // 2
    vmem = pl.BlockSpec(memory_space=pltpu.VMEM)
    hbm = pl.BlockSpec(memory_space=pl.ANY)
    dma = pltpu.SemaphoreType.DMA
    return pl.pallas_call(
        functools.partial(moe_kernel, n_dp),
        out_shape=jax.ShapeDtypeStruct((tokens, D), BF),
        in_specs=[vmem, vmem, vmem, vmem, hbm, hbm],
        out_specs=vmem,
        scratch_shapes=[
            pltpu.VMEM((n_dp, 8, tokens, D), BF),
            pltpu.VMEM(expert_in.shape, BF),
            pltpu.VMEM(expert_out.shape, BF),
            pltpu.VMEM((2, 4 * rows, D), BF),
            pltpu.VMEM((2, 4 * rows, FF), BF),
            pltpu.VMEM((n_dp, 8, rows, D), BF),
            pltpu.VMEM((n_dp, 8, rows, D), BF),
            pltpu.VMEM((n_dp, tokens, D), BF),
            pltpu.VMEM((n_dp, tokens, D), BF),
            dma((2,)),
            dma((n_dp + 1,)),
            dma((n_dp,)),
            dma((n_dp, 8)),
            dma((n_dp, 8)),
            dma((n_dp, 8)),
            dma((n_dp, 8)),
            dma((n_dp,)),
            dma((n_dp,)),
        ],
        compiler_params=pltpu.CompilerParams(
            collective_id=0, has_side_effects=True, vmem_limit_bytes=60 * 1024 * 1024
        ),
    )(expert_input, hidden_state, pick, weight, expert_in, expert_out)


def two_parts(a):
    high = lax.reduce_precision(a, 8, 7)
    return high.astype(BF), (a - high).astype(BF)


def slot_table(gate_rows, capacity):
    named = gate_rows > 0.0
    tokens = gate_rows.shape[-1]
    before = (
        jnp.arange(tokens, dtype=jnp.int32)[:, None] < jnp.arange(tokens, dtype=jnp.int32)[None, :]
    ).astype(BF)
    rank = jnp.einsum("...t,tu->...u", named.astype(BF), before, preferred_element_type=F32)
    slot = jnp.arange(capacity, dtype=jnp.int32).astype(F32)
    return named[..., None, :] & (rank[..., None, :] == slot[:, None])


def per_device(
    queries,
    key_in,
    value_in,
    gate_in,
    residual_in,
    log_decay,
    beta_logit,
    lengths,
    head_gain,
    out_proj,
    post_gain,
    expert_in,
    expert_out,
    routes,
    route_gates,
):
    tokens = queries.shape[1]
    n_ctx = lax.axis_size("ctx")
    n_dp = lax.axis_size("dp")
    local = expert_in.shape[0]
    devices = n_ctx * n_dp
    experts = local * devices
    capacity = tokens * TOPK * 6 // (5 * experts)
    group = HV // HK
    my_dp = lax.axis_index("dp")
    my_ctx = lax.axis_index("ctx")

    ids = jnp.arange(experts, dtype=jnp.int32)[:, None]
    gate_table = jnp.zeros((experts, tokens), F32)
    for k in range(TOPK):
        gate_table = gate_table + jnp.where(
            routes[0, :, k][None, :] == ids, route_gates[0, :, k][None, :], 0.0
        )
    gate_table = gate_table.astype(BF)
    column_gates = lax.all_gather(gate_table, "dp")

    beta = jax.nn.sigmoid(beta_logit[0])
    dh, dl = two_parts(log_decay[0])
    bh, bl = two_parts(beta)
    scal = jnp.stack([dh, dl, bh, bl]).reshape(4, n_ctx, group, tokens)
    scal = scal.transpose(1, 3, 0, 2).reshape(n_ctx, tokens, 4 * group)
    scal = jnp.pad(scal, ((0, 0), (0, 0), (0, SCAL - scal.shape[-1])))

    def by_head(a):
        return a[0].reshape(tokens, n_ctx, -1).transpose(1, 0, 2)

    sent = jnp.concatenate([by_head(queries), by_head(key_in), by_head(value_in), scal], -1)
    heads = lax.all_to_all(sent, "ctx", split_axis=0, concat_axis=0, tiled=True)
    mixed = mixer(lengths, heads.reshape(n_ctx * tokens, -1), head_gain)
    plane = column_gates.reshape(n_dp, n_dp, n_ctx, local, tokens)
    plane = lax.dynamic_index_in_dim(plane, my_dp, 1, False)
    gate_rows = plane.transpose(1, 0, 2, 3).reshape(n_ctx, -1, group * DV)
    extra = gate_rows.shape[1]
    gate_rows = jnp.pad(gate_rows, ((0, 0), (0, -extra % 16), (0, 0)))
    mixed = jnp.concatenate([mixed.reshape(n_ctx, tokens, group * DV), gate_rows], 1)
    mine = lax.all_to_all(mixed, "ctx", split_axis=0, concat_axis=0, tiled=True)
    my_gates = mine[:, tokens : tokens + extra].reshape(n_ctx, n_dp, local, tokens)
    my_gates = my_gates.transpose(1, 0, 2, 3)
    mine = mine[:, :tokens]
    unit = mine.transpose(1, 0, 2).reshape(tokens, HV * DV)
    normed = (unit.astype(F32) * jax.nn.silu(gate_in[0].astype(F32))).astype(BF)
    projected = jnp.dot(normed, out_proj, preferred_element_type=F32)
    hidden_state = (residual_in[0].astype(F32) + projected).astype(BF)
    expert_input = post_norm(hidden_state, post_gain)

    places = my_ctx ^ jnp.arange(n_ctx)
    my_gates = my_gates[:, places]
    pick = slot_table(my_gates, capacity).astype(BF)
    pick = pick.reshape(n_dp, n_ctx // 2, 2, local, capacity, tokens).transpose(0, 1, 3, 2, 4, 5)
    pick = pick[..., None, :] * jnp.eye(2, dtype=BF)[:, None, :, None]
    pick = pick.reshape(n_dp, n_ctx // 2, local * 2 * capacity, 2 * tokens)
    plane = plane[:, places]
    weight = jnp.where(slot_table(plane, capacity), plane[..., None, :], 0)
    weight = weight.reshape(n_dp, n_ctx * local * capacity, tokens).transpose(0, 2, 1)
    return moe(n_dp, expert_input, hidden_state, pick, weight, expert_in, expert_out)[None]


def solution(mesh):
    in_specs = (
        P("dp", "ctx", None),
        P("dp", "ctx", None),
        P("dp", "ctx", None),
        P("dp", "ctx", None),
        P("dp", "ctx", None),
        P("dp", None, "ctx"),
        P("dp", None, "ctx"),
        P("dp", None),
        P(),
        P(),
        P(),
        P(("dp", "ctx"), None, None),
        P(("dp", "ctx"), None, None),
        P("dp", "ctx", None),
        P("dp", "ctx", None),
    )
    out_specs = P("dp", "ctx", None)
    by_heads = mesh.shape["ctx"] == HK and mesh.shape["dp"] == 4
    return jax.shard_map(
        per_device if by_heads else per_device_long, mesh=mesh, in_specs=in_specs, out_specs=out_specs, check_vma=False
    )
```
